256 devices in a mesh: ctx: 4 (over x), tp: 8 (over y, z_hi), dp: 8 (over z_lo, core).
Axes of the slice: x: 4, y: 4, z: 8 (z_hi: 2, z_lo: 4; z = z_hi * 4 + z_lo), core: 2. Of those that a mesh axis runs over, the one named last changes fastest.
Arguments:
- residual: bfloat16 [32768, 4096], P(('dp', 'ctx', 'tp')), parts along dimension 0, may hold values from -6 to 6
- queries: bfloat16 [32768, 4096], P(('dp', 'ctx'), 'tp'), parts along dimension 0, may hold values from -5 to 5
- key_value: bfloat16 [2, 32768, 512], P(None, ('dp', 'ctx'), 'tp'), parts along dimension 1, may hold values from -5 to 5
- out_proj: bfloat16 [4096, 4096], P('tp', 'ctx'), may hold values from -0.5 to 0.5
- norm_gain: float32 [4096], replicated, may hold values from 0.1 to 1.9
- expert_ids: int32 [32768, 8], P(('dp', 'ctx', 'tp')), parts along dimension 0, may hold values from 0 to 127, all different within a row; in each aligned block of 128 rows (0 to 127, 128 to 255, ...) at most 24 rows name the same one
- gate_weights: float32 [32768, 8], P(('dp', 'ctx', 'tp')), parts along dimension 0, may hold values from 0.2 to 1
- expert_in: bfloat16 [4, 2, 4096, 1536], P('ctx', None, None, 'tp'), may hold values from -0.09375 to 0.09375
- expert_down: bfloat16 [4, 1536, 4096], P('ctx', 'tp'), may hold values from -0.15625 to 0.15625
Outputs:
- layer_out: bfloat16 [32768, 4096], P(('dp', 'ctx', 'tp')), parts along dimension 0
The draws below stay inside these ranges and needn't reach their ends.
There are 8 independent parts, one for each index of `dp`. The reference program is written for one: setup_inputs(seed, part) draws one part's arguments, and reference() takes and returns one part's arrays. A program takes and returns all parts, laid end to end along the dimension named above; an argument that names none is the same for every part. Nothing has to cross between parts.
Inputs may be any that keep to these rules, and one draw needn't show every extreme that they name: `expert_ids`: each row names 8 different experts; in the rows of one device no expert is named more than 24 times.
All inputs are finite; a program needn't handle non-finite values.
Results may differ from the reference program's by a relative error of at most 0.017.
Values may be sent and summed in bfloat16 or wider, within the bound.
A program may use at most 64 MiB of HBM per device.

```python
import math
import jax
import jax.numpy as jnp
import numpy as np
from jax import lax

D = 4096
HEADS = 32
KV = 4
HD = 128
EXPERTS = 128
TOP = 8
EHID = 1536
TOK_DEV = 128
TOKENS = 4096
WIN_EXP = 4
CAP = 24
N_CTX = 4
N_TP = 8


def draw_queries(key, part):
    key = jax.random.fold_in(key, 7)
    values = jnp.clip(1.5 * jax.random.normal(key, (TOKENS, HEADS, HD), jnp.float32), -5.0, 5.0)
    return values.reshape(TOKENS, HEADS * HD).astype(jnp.bfloat16)


def draw_key_value(key, part):
    key = jax.random.fold_in(key, 9)
    values = jnp.clip(jax.random.normal(key, (2, TOKENS, KV, HD), jnp.float32), -5.0, 5.0)
    return values.reshape(2, TOKENS, KV * HD).astype(jnp.bfloat16)


def level_of(rng, extent, split, low, top_value):
    factor_of = 1.0
    for axis_at, parts in split:
        steps = jax.random.uniform(jax.random.fold_in(jax.random.fold_in(rng, 6), axis_at), (parts,), jnp.float32, low / len(split), top_value / len(split))
        factor_of = factor_of * jnp.repeat(jnp.exp(steps), extent[axis_at] // parts).reshape((-1,) + (1,) * (len(extent) - 1 - axis_at))
    return factor_of


def deal_out(rng, own, number, rows, count, top, most, lean):
    sequence = jax.random.permutation(rng, count)
    packed, ordinary = shares(count, rows * top, most, lean, True), shares(count, rows * top, most, lean, False)
    places = jnp.arange(count)

    def named(lengths, offset_by):
        used = int((lengths > 0).sum())
        fixed = max(1, used // 4)
        moved = fixed + (places - fixed + offset_by * (used - fixed)) % max(1, count - fixed)
        return jnp.zeros((count,), jnp.int32).at[sequence[jnp.where(places < fixed, places, moved)]].set(jnp.asarray(lengths, jnp.int32))

    lengths = jnp.where(number % 4 == 0, named(packed, number // 4), named(ordinary, number - number // 4 - 1))
    mixed = jax.random.permutation(jax.random.fold_in(own, 3), count)
    giver, receiver = mixed[0:count // 2 * 2:2], mixed[1:count // 2 * 2:2]
    room = jnp.minimum(lengths[giver] - 1, most - lengths[receiver]) // 2
    room = jnp.where((giver == sequence[0]) | (receiver == sequence[0]) | (lengths[receiver] == 0), 0, jnp.maximum(room, 0))
    moved = jax.random.randint(jax.random.fold_in(own, 4), (count // 2,), 0, 1 << 20) % (room + 1)
    lengths = lengths.at[giver].add(-moved).at[receiver].add(moved)
    members = jnp.searchsorted(jnp.cumsum(lengths), jnp.arange(rows * top), side="right").astype(jnp.int32)
    listing = members.reshape(top, rows).T
    listing = listing[jax.random.permutation(jax.random.fold_in(own, 1), rows)]
    offset_by = jax.random.randint(jax.random.fold_in(own, 2), (rows, 1), 0, top)
    return jnp.take_along_axis(listing, (jnp.arange(top)[None, :] + offset_by) % top, axis=1)


def shares(amount, total, most, skew, full):
    weights = [(1 << 20) // math.isqrt(grade ** skew) + 1 for grade in range(1, amount + 1)]
    largest = most if full else min(most, max(-(-total // amount), total * weights[0] // sum(weights)))
    least = 1 if total - largest >= amount - 1 else 0
    given, surplus = [largest] + [least] * (amount - 1), total - largest - least * (amount - 1)
    while surplus > 0:
        candidates = [i for i in range(1, amount) if given[i] < largest] or [i for i in range(1, amount) if given[i] < most]
        mass, budget = sum([weights[i] for i in candidates]), surplus
        for i in candidates:
            more = min(most - given[i], max(1, budget * weights[i] // mass), surplus)
            given[i] = given[i] + more
            surplus = surplus - more
    return np.array(given)


def centred(own_key, extent, width, reach, shards=(), kind=jnp.bfloat16):
    level = level_of(own_key, extent, shards, -0.22, 0.18) if shards else 1.0
    array = jax.random.normal(own_key, extent, jnp.float32) * width * level
    return jnp.minimum(jnp.maximum(array, -reach), reach).astype(kind)


def setup_inputs(seed: int = 0, part: int = 0) -> dict:
    key_of = jax.random.split(jax.random.key(seed), 10)
    own_keys = jax.random.split(jax.random.fold_in(key_of[9], part), 10)
    residual = centred(own_keys[0], (TOKENS, D), 1.0, 6.0, ((0, 32),))
    queries = draw_queries(jax.random.fold_in(jax.random.fold_in(key_of[9], part), 71), part)
    key_value = draw_key_value(jax.random.fold_in(jax.random.fold_in(key_of[9], part), 71), part)
    out_proj = centred(key_of[3], (HEADS * HD, D), HD ** -0.5, 0.5, ((0, 8), (1, 4)))
    norm_gain = jnp.clip(1.0 + 0.18 * jax.random.normal(key_of[4], (D,), jnp.float32), 0.1, 1.9)
    expert_ids_keys = jax.random.split(jax.random.fold_in(own_keys[5], 1), TOKENS // TOK_DEV)
    expert_ids_turns = jax.random.permutation(jax.random.fold_in(own_keys[5], 3), TOKENS // TOK_DEV)
    expert_ids = jax.vmap(lambda own, number: deal_out(jax.random.fold_in(own_keys[5], 2), own, number, TOK_DEV, EXPERTS, TOP, CAP, 2))(expert_ids_keys, expert_ids_turns).reshape((TOKENS, TOP))
    gate_weights = jnp.clip(0.2 + 0.8 * jax.random.uniform(own_keys[6], (TOKENS, TOP), jnp.float32) ** level_of(own_keys[6], (TOKENS, TOP), ((0, 32),), -0.2, 0.2), 0.2, 1.0)
    expert_in = centred(key_of[7], (WIN_EXP, 2, D, EHID), D ** -0.5, 0.09375, ((0, 4), (3, 8)))
    expert_down = centred(key_of[8], (WIN_EXP, EHID, D), EHID ** -0.5, 0.15625, ((0, 4), (1, 8)))
    return {"residual": residual, "queries": queries, "key_value": key_value, "out_proj": out_proj, "norm_gain": norm_gain, "expert_ids": expert_ids, "gate_weights": gate_weights, "expert_in": expert_in, "expert_down": expert_down}


def attention(queries, key_value):
    group_size = HEADS // KV
    score_scale = HD ** (-0.5)
    query_heads = queries.reshape(TOKENS, HEADS, HD).transpose(1, 0, 2)
    key_heads = key_value[0].reshape(TOKENS, KV, HD).transpose(1, 0, 2)
    value_heads = key_value[1].reshape(TOKENS, KV, HD).transpose(1, 0, 2)
    positions = jnp.arange(TOKENS, dtype=jnp.int32)
    allowed = positions[None, :] <= positions[:, None]

    def one_head(head_index):
        query_rows = query_heads[head_index]
        key_rows = key_heads[head_index // group_size]
        value_rows = value_heads[head_index // group_size]
        scores = jnp.dot(query_rows, key_rows.T, preferred_element_type=jnp.float32) * score_scale
        scores = jnp.where(allowed, scores, -1e+30)
        row_max = lax.optimization_barrier(jnp.max(scores, axis=1, keepdims=True))
        weights = jnp.exp(scores - row_max)
        totals = lax.optimization_barrier(jnp.sum(weights, axis=1, keepdims=True))
        mixed_out = jnp.dot(weights.astype(jnp.bfloat16), value_rows, preferred_element_type=jnp.float32)
        return (mixed_out / totals).astype(jnp.bfloat16)
    outputs = lax.map(one_head, jnp.arange(HEADS, dtype=jnp.int32))
    return outputs.transpose(1, 0, 2).reshape(TOKENS, HEADS * HD)

def project(attended, out_proj):
    slice_rows = HEADS * HD // N_TP

    def one_slice(running, slice_index):
        row_block = lax.dynamic_slice_in_dim(attended, slice_index * slice_rows, slice_rows, 1)
        weight_rows = lax.dynamic_slice_in_dim(out_proj, slice_index * slice_rows, slice_rows, 0)
        part_sum = jnp.dot(row_block, weight_rows, preferred_element_type=jnp.float32).astype(jnp.bfloat16)
        return (running + lax.optimization_barrier(part_sum).astype(jnp.float32), None)
    running, _ = lax.scan(one_slice, jnp.zeros((TOKENS, D), jnp.float32), jnp.arange(N_TP, dtype=jnp.int32))
    return running

def experts(normed, expert_ids, gate_weights, expert_in, expert_down):
    rows_cap = CAP * N_CTX * N_TP
    slice_width = EHID // N_TP

    def one_expert(running, expert):
        matches = expert_ids == expert
        chosen_any = jnp.any(matches, axis=1)
        row_order = jnp.argsort(jnp.where(chosen_any, 0, 1).astype(jnp.int32), stable=True)[:rows_cap].astype(jnp.int32)
        row_block = normed[row_order]
        gate_part = jnp.dot(row_block, expert_in[expert, 0], preferred_element_type=jnp.float32)
        up_part = jnp.dot(row_block, expert_in[expert, 1], preferred_element_type=jnp.float32)
        hidden = (jax.nn.silu(gate_part) * up_part).astype(jnp.bfloat16)
        down_rows = expert_down[expert]

        def one_slice(partial_sum, slice_index):
            hidden_slice = lax.dynamic_slice_in_dim(hidden, slice_index * slice_width, slice_width, 1)
            down_slice = lax.dynamic_slice_in_dim(down_rows, slice_index * slice_width, slice_width, 0)
            part_sum = jnp.dot(hidden_slice, down_slice, preferred_element_type=jnp.float32).astype(jnp.bfloat16)
            return (partial_sum + lax.optimization_barrier(part_sum).astype(jnp.float32), None)
        expert_sum, _ = lax.scan(one_slice, jnp.zeros((rows_cap, D), jnp.float32), jnp.arange(N_TP, dtype=jnp.int32))
        expert_sum = lax.optimization_barrier(expert_sum.astype(jnp.bfloat16)).astype(jnp.float32)
        row_weight = lax.optimization_barrier(jnp.sum(jnp.where(matches, gate_weights, 0.0), axis=1))[row_order]
        return (running.at[row_order].add(row_weight[:, None] * expert_sum), None)
    running, _ = lax.scan(one_expert, jnp.zeros((TOKENS, D), jnp.float32), jnp.arange(WIN_EXP, dtype=jnp.int32))
    return running

def reference(residual, queries, key_value, out_proj, norm_gain, expert_ids, gate_weights, expert_in, expert_down):
    attended = attention(queries, key_value)
    stream = (residual.astype(jnp.float32) + project(attended, out_proj)).astype(jnp.bfloat16)
    stream_wide = lax.optimization_barrier(stream).astype(jnp.float32)
    mean_square = lax.optimization_barrier(jnp.mean(stream_wide * stream_wide, axis=1, keepdims=True))
    normed = (stream_wide * lax.rsqrt(mean_square + 1e-06) * norm_gain).astype(jnp.bfloat16)
    added = experts(normed, expert_ids, gate_weights, expert_in, expert_down)
    return (stream_wide + added).astype(jnp.bfloat16)
```

```python
import jax
import jax.numpy as jnp
from jax import lax
from jax.experimental import pallas as pl
from jax.experimental.pallas import tpu as pltpu
from jax.sharding import PartitionSpec as P

HD = 128
CAP = 24
D = 4096
HALF = D // 2
NX = 4
NY = 4
ROWS = 128
EROWS = NX * CAP
MESH = pl.DeviceIdType.MESH
BF = jnp.bfloat16
F32 = jnp.float32
SCALE2 = HD ** (-0.5) * 1.4426950408889634
NT = (((1,), (1,)), ((), ()))


def kernel(
    q_ref, kv_ref, w_ref, res_ref, gain_ref, ids_ref, gw_ref, ein_ref, ed_ref,
    out_ref,
    kvbuf, vext, q2, qown, qother, acc, mrow, att, wbuf, sbuf, rsbuf, stream,
    packed, xd, disp, down, ret, xsend, eb, einbuf, edbuf,
    loc, s_kv, r_kvz, r_kvx, s_q, r_q, s_w, r_wz, r_wx, r_ws,
    s_rs, r_rs, s_e, r_e, s_x, r_x, s_y, r_y, s_ry, r_ry, s_rx, r_rx,
):
    c = lax.axis_index("ctx")
    t = lax.axis_index("tp")
    d = lax.axis_index("dp")
    y = t // 2
    h = t % 2
    k = d % 2
    hp = 1 - h
    kp = 1 - k

    pair = {"ctx": c, "tp": 2 * y + hp, "dp": d}
    sib = {"ctx": c, "tp": t, "dp": d + 1 - 2 * k}

    def xpeer(o):
        return {"ctx": lax.rem(c + o, NX), "tp": t, "dp": d}

    def ypeer(o):
        return {"ctx": c, "tp": 2 * lax.rem(y + o, NY) + h, "dp": d}

    def rcopy(src, dst, ss, rs, dev):
        return pltpu.make_async_remote_copy(
            src_ref=src, dst_ref=dst, send_sem=ss, recv_sem=rs, device_id=dev, device_id_type=MESH
        )

    barrier = pltpu.get_barrier_semaphore()
    peers = [pair, sib] + [xpeer(o) for o in (1, 2, 3)] + [ypeer(o) for o in (1, 2, 3)]
    for dev in peers:
        pl.semaphore_signal(barrier, inc=1, device_id=dev, device_id_type=MESH)
    pl.semaphore_wait(barrier, len(peers))

    kv_pair = rcopy(kv_ref, kvbuf.at[c, :, h], s_kv.at[0], r_kvz, pair)
    kv_pair.start()

    def kv_own(o):
        return rcopy(kv_ref, kvbuf.at[c, :, h], s_kv.at[o], r_kvx.at[o - 1, 0], xpeer(o))

    def kv_fwd(o):
        return rcopy(
            kvbuf.at[c, :, hp], kvbuf.at[c, :, hp], s_kv.at[3 + o], r_kvx.at[o - 1, 1], xpeer(o)
        )

    for o in (1, 2, 3):
        pl.when(c + o < NX)(lambda o=o: kv_own(o).start())
    kv_loc = pltpu.make_async_copy(kv_ref, kvbuf.at[c, :, h], loc.at[0])
    kv_loc.start()
    q_loc = pltpu.make_async_copy(q_ref.at[:, h], qown, loc.at[1])
    q_loc.start()
    w_loc = pltpu.make_async_copy(w_ref, wbuf.at[h, c], loc.at[2])
    w_loc.start()
    ein_loc = pltpu.make_async_copy(ein_ref, einbuf.at[:, h], loc.at[3])
    ein_loc.start()
    ed_loc = pltpu.make_async_copy(ed_ref, edbuf.at[h], loc.at[4])
    ed_loc.start()

    vext[:, :, HD:] = jnp.ones((NX, 1024, HD), BF)

    def spread_q(src, which):
        for b in range(4):
            block = src[b]
            for j in range(4):
                q2[which, j, b] = block[:, j * HD : (j + 1) * HD]

    q_loc.wait()
    spread_q(qown, h)

    q_pair = rcopy(q_ref.at[:, hp], qother, s_q, r_q, pair)
    kv_loc.wait()
    kv_pair.wait_recv()
    q_pair.start()
    for o in (1, 2, 3):
        pl.when(c + o < NX)(lambda o=o: kv_fwd(o).start())

    def put_v(src):
        vext[src, :, :HD] = kvbuf[src, 1].reshape(HD, 1024).astype(F32).T.astype(BF)

    put_v(c)
    w_pair = rcopy(w_ref.at[k], wbuf.at[h, c, k], s_w.at[0], r_wz, pair)

    def w_own(o):
        return rcopy(w_ref.at[k], wbuf.at[h, c, k], s_w.at[o], r_wx.at[o - 1, 0], xpeer(o))

    def w_fwd(o):
        return rcopy(
            wbuf.at[hp, c, k], wbuf.at[hp, c, k], s_w.at[3 + o], r_wx.at[o - 1, 1], xpeer(o)
        )

    w_sib = rcopy(wbuf.at[hp, c, k], wbuf.at[hp, c, k], s_w.at[7], r_ws.at[0], sib)

    def w_sib_own(o):
        cs = lax.rem(c + NX - o, NX)
        return rcopy(wbuf.at[h, cs, k], wbuf.at[h, cs, k], s_w.at[7 + o], r_ws.at[o], sib)

    def w_sib_fwd(o):
        cs = lax.rem(c + NX - o, NX)
        return rcopy(wbuf.at[hp, cs, k], wbuf.at[hp, cs, k], s_w.at[10 + o], r_ws.at[3 + o], sib)

    ein_pair = rcopy(ein_ref.at[k], einbuf.at[k, h], s_e.at[0], r_e.at[0], pair)
    ed_pair = rcopy(ed_ref.at[k], edbuf.at[h, k], s_e.at[1], r_e.at[1], pair)
    ein_sib = rcopy(einbuf.at[k, hp], einbuf.at[k, hp], s_e.at[2], r_e.at[2], sib)
    ed_sib = rcopy(edbuf.at[hp, k], edbuf.at[hp, k], s_e.at[3], r_e.at[3], sib)

    row_at = lax.broadcasted_iota(jnp.int32, (4, ROWS, 256), 1).reshape(4 * ROWS, 256) + h * ROWS
    col_at = lax.broadcasted_iota(jnp.int32, (4 * ROWS, 256), 1)
    allowed = col_at <= row_at

    def diagonal(which):
        keys = kvbuf[c, 0].reshape(HD, 1024)
        for b in range(4):
            kl = (b + 1) * 256
            qs = q2[which, :, b].reshape(4 * ROWS, HD)
            s = jnp.dot(qs, keys[:, :kl], preferred_element_type=F32)
            last = jnp.where(allowed, s[:, kl - 256 :], -1e30)
            s = last if b == 0 else jnp.concatenate([s[:, : kl - 256], last], axis=1)
            top = jnp.broadcast_to(jnp.max(s, axis=1, keepdims=True) * SCALE2, (4 * ROWS, HD))
            p = jnp.exp2(s * SCALE2 - jnp.concatenate([top] * (kl // HD), axis=1)).astype(BF)
            acc[which, :, b] = jnp.dot(
                p, vext[c, :kl], preferred_element_type=F32
            ).reshape(4, ROWS, 2 * HD)
            mrow[which, :, b] = top.reshape(4, ROWS, HD)

    def full_block(which, src):
        keys = kvbuf[src, 0].reshape(HD, 1024)
        for j in range(4):
            qs = q2[which, j].reshape(4 * ROWS, HD)
            s = jnp.dot(qs, keys, preferred_element_type=F32)
            old = mrow[which, j].reshape(4 * ROWS, HD)
            top = jnp.maximum(old, jnp.max(s, axis=1, keepdims=True) * SCALE2)
            factor = jnp.exp2(old - top)
            p = jnp.exp2(s * SCALE2 - jnp.concatenate([top] * 8, axis=1)).astype(BF)
            update = jnp.dot(p, vext[src], preferred_element_type=F32)
            acc[which, j] = (
                acc[which, j].reshape(4 * ROWS, 2 * HD) * jnp.concatenate([factor] * 2, axis=1)
                + update
            ).reshape(4, ROWS, 2 * HD)
            mrow[which, j] = top.reshape(4, ROWS, HD)

    def group(g, carry):
        which = lax.rem(h + g, 2)

        @pl.when(g == 1)
        def _():
            q_pair.wait_recv()
            spread_q(qother, hp)
            w_pair.start()
            ein_pair.start()
            ed_pair.start()

        diagonal(which)

        @pl.when(g == 0)
        def _():
            for o in (1, 3, 2):
                w_own(o).start()

        def earlier(o, carry):
            src = c - o

            @pl.when(g == 0)
            def _():
                rcopy(
                    kv_ref, kvbuf.at[src, :, h], s_kv.at[o], r_kvx.at[o - 1, 0], xpeer(o)
                ).wait_recv()
                rcopy(
                    kv_ref, kvbuf.at[src, :, hp], s_kv.at[o], r_kvx.at[o - 1, 1], xpeer(o)
                ).wait_recv()
                put_v(src)

            full_block(which, src)
            return carry

        lax.fori_loop(1, c + 1, earlier, 0)
        return carry

    lax.fori_loop(0, 2, group, 0)

    for w in range(2):
        for j in range(4):
            whole = acc[w, j].reshape(4 * ROWS, 2 * HD)
            head = (whole[:, :HD] / whole[:, HD:]).astype(BF)
            att[:, :, (4 * w + j) * HD : (4 * w + j + 1) * HD] = head.reshape(4, ROWS, HD)

    w_pair.wait_recv()
    w_sib.start()
    for o in (1, 3, 2):
        w_fwd(o).start()
    for o in (1, 3, 2):
        w_own(o).wait_recv()
        w_sib_own(o).start()
    w_loc.wait()
    w_sib.wait_recv()

    def rs_copy(i, o):
        return rcopy(
            sbuf.at[i, lax.rem(y + o, NY)], rsbuf.at[o - 1, i], s_rs.at[i, o - 1],
            r_rs.at[i, o - 1], ypeer(o),
        )

    order = (0, 1, 3, 2)
    for i, o in enumerate(order):
        cs = lax.rem(c + NX - o, NX)
        if o:
            w_fwd(o).wait_recv()
            w_sib_fwd(o).start()
            w_sib_own(o).wait_recv()
            w_sib_fwd(o).wait_recv()

        def tile(n, carry, cs=cs, i=i):
            at = pl.ds(pl.multiple_of(n * 256, 256), 256)
            rows = att[...].reshape(4 * ROWS, 1024)
            w0 = jnp.concatenate([wbuf[0, cs, 0, :, at], wbuf[0, cs, 1, :, at]], axis=0)
            w1 = jnp.concatenate([wbuf[1, cs, 0, :, at], wbuf[1, cs, 1, :, at]], axis=0)
            part = jnp.dot(rows[:, :512], w0, preferred_element_type=F32)
            part = part + jnp.dot(rows[:, 512:], w1, preferred_element_type=F32)
            sbuf[i, :, :, at] = part.astype(BF).reshape(4, ROWS, 256)
            return carry

        lax.fori_loop(0, 4, tile, 0)
        for o2 in (2, 1, 3):
            rs_copy(i, o2).start()

    slot_at = lax.broadcasted_iota(jnp.int32, (ROWS, ROWS), 0)
    lane_at = lax.broadcasted_iota(jnp.int32, (ROWS, ROWS), 1)
    group_at = sum((slot_at >= n * CAP).astype(jnp.int32) for n in (1, 2, 3, 4))
    expert_at = group_at + c
    expert_at = jnp.where(expert_at >= NX, expert_at - NX, expert_at)
    expert_at = jnp.where(group_at == 4, -1, expert_at)
    match = jnp.zeros((ROWS, ROWS), F32)
    gate = jnp.zeros((ROWS, ROWS), F32)
    for n in range(8):
        hit = ids_ref[n : n + 1, :] == expert_at
        match = match + jnp.where(hit, 1.0, 0.0)
        gate = gate + jnp.where(hit, gw_ref[n : n + 1, :], 0.0)
    before = jnp.where(slot_at < lane_at, 1.0, 0.0).astype(BF)
    rank = jnp.dot(match.astype(BF), before, preferred_element_type=F32)
    want = (slot_at - group_at * CAP).astype(F32)
    chosen = jnp.where(rank == want, match, 0.0)
    weighted = (chosen * gate).T
    chosen = chosen.astype(BF)

    square = jnp.zeros((ROWS, 1), F32)
    for i, o in enumerate(order):
        cs = lax.rem(c + NX - o, NX)
        at = pl.ds(pl.multiple_of(cs * 1024, 1024), 1024)
        for o2 in (1, 2, 3):
            rs_copy(i, o2).wait_recv()
        total = sbuf[i, y].astype(F32)
        for o2 in (1, 2, 3):
            total = total + rsbuf[o2 - 1, i].astype(F32)
        block = (res_ref[:, at].astype(F32) + total).astype(BF)
        stream[:, at] = block
        wide = block.astype(F32)
        square = square + jnp.sum(wide * wide, axis=1, keepdims=True)
    inv = lax.rsqrt(square * (1.0 / D) + 1e-6)

    for half in range(2):
        for n in range(4):
            lo = half * HALF + n * 512
            normed = (
                stream[:, lo : lo + 512].astype(F32) * inv * gain_ref[:, lo : lo + 512]
            ).astype(BF)
            rows = jnp.dot(chosen, normed, preferred_element_type=F32)
            for o in range(NX):
                if half == 0:
                    xsend[o, :CAP, n * 512 : (n + 1) * 512] = rows[o * CAP : (o + 1) * CAP]
                else:
                    xsend[o, CAP:, n * 512 : (n + 1) * 512] = rows[o * CAP : (o + 1) * CAP]
    packed[...] = xsend[...].astype(BF)

    def x_copy(o):
        return rcopy(packed.at[o], xd.at[o - 1], s_x.at[o - 1], r_x.at[o - 1], xpeer(o))

    for o in (2, 1, 3):
        x_copy(o).start()
    ein_pair.wait_recv()
    ein_sib.start()
    for o in (1, 3, 2):
        x_copy(o).wait_recv()
    pieces = [packed[0].astype(F32)] + [xd[o - 1].astype(F32) for o in (1, 2, 3)]
    for half in range(2):
        rows = jnp.concatenate([p[half * CAP : (half + 1) * CAP] for p in pieces], axis=0)
        disp[0, :, half * HALF : (half + 1) * HALF] = rows.astype(BF)

    def y_copy(o):
        return rcopy(disp.at[0], disp.at[o], s_y.at[o - 1], r_y.at[o - 1], ypeer(o))

    for o in (2, 1, 3):
        y_copy(o).start()
    ed_pair.wait_recv()
    ed_sib.start()
    ein_loc.wait()
    ed_loc.wait()
    ein_sib.wait_recv()
    ed_sib.wait_recv()
    for o in (1, 3, 2):
        y_copy(o).wait_recv()

    def project_in(n):
        total = jnp.zeros((4 * EROWS, 384), F32)
        for kk in range(4):
            at = slice(kk * 1024, (kk + 1) * 1024)
            total = total + lax.dot_general(
                disp[:, :, at].reshape(4 * EROWS, 1024),
                einbuf[n, :, :, at].reshape(384, 1024),
                NT,
                preferred_element_type=F32,
            )
        return total

    gate_part = project_in(0)
    hidden = (gate_part / (1.0 + jnp.exp(-gate_part)) * project_in(1)).astype(BF)

    def down_tile(n, carry):
        at = pl.ds(pl.multiple_of(n * 512, 512), 512)
        weights = edbuf[:, :, :, at].reshape(384, 512)
        part = jnp.dot(hidden, weights, preferred_element_type=F32)
        down[:, :, at] = part.astype(BF).reshape(4, EROWS, 512)
        return carry

    lax.fori_loop(0, D // 512, down_tile, 0)

    def ry_copy(o):
        return rcopy(
            down.at[o], ret.at[o - 1], s_ry.at[o - 1], r_ry.at[o - 1], ypeer(NY - o)
        )

    for o in (2, 1, 3):
        ry_copy(o).start()
    for o in (1, 3, 2):
        ry_copy(o).wait_recv()
    for half in range(2):
        at = slice(half * HALF, (half + 1) * HALF)
        total = down[0, :, at].astype(F32)
        for o in (1, 2, 3):
            total = total + ret[o - 1, :, at].astype(F32)
        for o in range(NX):
            xsend[o, half * CAP : (half + 1) * CAP, :] = total[o * CAP : (o + 1) * CAP]
    x_copy(1).wait_send()
    x_copy(2).wait_send()
    x_copy(3).wait_send()
    packed[...] = xsend[...].astype(BF)

    def rx_copy(o):
        return rcopy(packed.at[o], eb.at[o - 1], s_rx.at[o - 1], r_rx.at[o - 1], xpeer(NX - o))

    for o in (2, 1, 3):
        rx_copy(o).start()
    high = weighted.astype(BF)
    rest = weighted - high.astype(F32)
    mid = rest.astype(BF)
    low = (rest - mid.astype(F32)).astype(BF)
    for o in (1, 3, 2):
        rx_copy(o).wait_recv()
    pieces = [packed[0].astype(F32)] + [eb[o - 1].astype(F32) for o in (1, 2, 3)]
    for half in range(2):
        at = slice(half * HALF, (half + 1) * HALF)
        rows = jnp.concatenate(
            [p[half * CAP : (half + 1) * CAP] for p in pieces]
            + [jnp.zeros((ROWS - EROWS, HALF), F32)],
            axis=0,
        ).astype(BF)
        added = (
            jnp.dot(high, rows, preferred_element_type=F32)
            + jnp.dot(mid, rows, preferred_element_type=F32)
            + jnp.dot(low, rows, preferred_element_type=F32)
        )
        out_ref[:, at] = (stream[:, at].astype(F32) + added).astype(BF)

    kv_pair.wait_send()
    for o in (1, 2, 3):

        @pl.when(c + o < NX)
        def _(o=o):
            kv_own(o).wait_send()
            kv_fwd(o).wait_send()

    q_pair.wait_send()
    w_pair.wait_send()
    w_sib.wait_send()
    for o in (1, 2, 3):
        w_own(o).wait_send()
        w_fwd(o).wait_send()
        w_sib_own(o).wait_send()
        w_sib_fwd(o).wait_send()
        for i in range(4):
            rs_copy(i, o).wait_send()
        y_copy(o).wait_send()
        ry_copy(o).wait_send()
        rx_copy(o).wait_send()
    ein_pair.wait_send()
    ed_pair.wait_send()
    ein_sib.wait_send()
    ed_sib.wait_send()


def body(residual, queries, key_value, out_proj, norm_gain, expert_ids, gate_weights, expert_in, expert_down):
    sem = pltpu.SemaphoreType.DMA
    vmem = pl.BlockSpec(memory_space=pltpu.VMEM)
    hbm = pl.BlockSpec(memory_space=pl.ANY)
    scratch = [
        pltpu.VMEM((NX, 2, 2, 64, 1024), BF),
        pltpu.VMEM((NX, 1024, 2 * HD), BF),
        pltpu.VMEM((2, 4, 4, ROWS, HD), BF),
        pltpu.VMEM((4, ROWS, 512), BF),
        pltpu.VMEM((4, ROWS, 512), BF),
        pltpu.VMEM((2, 4, 4, ROWS, 2 * HD), F32),
        pltpu.VMEM((2, 4, 4, ROWS, HD), F32),
        pltpu.VMEM((4, ROWS, 1024), BF),
        pltpu.VMEM((2, NX, 2, 256, 1024), BF),
        pltpu.VMEM((4, NY, ROWS, 1024), BF),
        pltpu.VMEM((3, 4, ROWS, 1024), BF),
        pltpu.VMEM((ROWS, D), BF),
        pltpu.VMEM((NX, 2 * CAP, HALF), BF),
        pltpu.VMEM((3, 2 * CAP, HALF), BF),
        pltpu.VMEM((NY, EROWS, D), BF),
        pltpu.VMEM((NY, EROWS, D), BF),
        pltpu.VMEM((3, EROWS, D), BF),
        pltpu.VMEM((NX, 2 * CAP, HALF), F32),
        pltpu.VMEM((3, 2 * CAP, HALF), BF),
        pltpu.VMEM((2, 2, 192, D), BF),
        pltpu.VMEM((2, 2, 96, D), BF),
        sem((5,)),
        sem((7,)), sem, sem((3, 2)),
        sem, sem,
        sem((14,)), sem, sem((3, 2)), sem((7,)),
        sem((4, 3)), sem((4, 3)),
        sem((4,)), sem((4,)),
        sem((3,)), sem((3,)), sem((3,)), sem((3,)),
        sem((3,)), sem((3,)), sem((3,)), sem((3,)),
    ]
    return pl.pallas_call(
        kernel,
        out_shape=jax.ShapeDtypeStruct((ROWS, D), BF),
        in_specs=[hbm, hbm, hbm, vmem, vmem, vmem, vmem, hbm, hbm],
        out_specs=vmem,
        scratch_shapes=scratch,
        compiler_params=pltpu.CompilerParams(
            collective_id=0, has_side_effects=True, vmem_limit_bytes=62 * 1024 * 1024
        ),
        name="layer",
    )(
        queries.reshape(4, 2, ROWS, 512),
        jnp.swapaxes(key_value, 1, 2),
        out_proj.reshape(2, 256, 1024),
        residual,
        norm_gain.reshape(1, D),
        expert_ids.T,
        gate_weights.T,
        jnp.swapaxes(expert_in[0], 1, 2),
        expert_down[0].reshape(2, 96, D),
    )


def solution(mesh):
    in_specs = (
        P(("dp", "ctx", "tp"), None),
        P(("dp", "ctx"), "tp"),
        P(None, ("dp", "ctx"), "tp"),
        P("tp", "ctx"),
        P(),
        P(("dp", "ctx", "tp"), None),
        P(("dp", "ctx", "tp"), None),
        P("ctx", None, None, "tp"),
        P("ctx", "tp", None),
    )
    out_specs = P(("dp", "ctx", "tp"), None)
    return jax.shard_map(body, mesh=mesh, in_specs=in_specs, out_specs=out_specs, check_vma=False)
```

```python
import jax
import jax.numpy as jnp
from jax import lax
from jax.experimental import pallas as pl
from jax.experimental.pallas import tpu as pltpu
from jax.sharding import PartitionSpec as P

HD = 128
CAP = 24
D = 4096
HALF = D // 2
NX = 4
NY = 4
ROWS = 128
EROWS = NX * CAP
MESH = pl.DeviceIdType.MESH
BF = jnp.bfloat16
F32 = jnp.float32
SCALE2 = HD ** (-0.5) * 1.4426950408889634
NT = (((1,), (1,)), ((), ()))


def kernel(
    q_ref, kv_ref, w_ref, res_ref, gain_ref, ids_ref, gw_ref, ein_ref, ed_ref,
    out_ref,
    kvbuf, vext, q2, qown, qother, acc, mrow, att, wbuf, sbuf, oph, rsbuf, stream,
    xsend, packed, xd, disp, down, rop, rnb, back, eb, einbuf, edbuf,
    loc, s_kv, r_kvz, r_kvx, s_q, r_q, s_w, r_wz, r_wx, r_ws,
    s_op, r_op, s_rs, r_rs, s_e, r_e, s_sib, r_sib, s_x, r_x, s_y, r_y, s_yp, r_yp,
    s_ro, r_ro, s_rn, r_rn, s_rx, r_rx,
):
    c = lax.axis_index("ctx")
    t = lax.axis_index("tp")
    d = lax.axis_index("dp")
    y = t // 2
    h = t % 2
    k = d % 2
    hp = 1 - h
    kp = 1 - k

    zl = d // 2
    edge = (zl == 0) | (zl == 3)
    pair = {"ctx": c, "tp": 2 * y + hp, "dp": d}
    sib = {"ctx": c, "tp": t, "dp": d + 1 - 2 * k}
    across = {"ctx": c, "tp": 2 * y + hp, "dp": (3 - zl) * 2 + k}
    inner = {"ctx": c, "tp": t, "dp": (zl + 1 - 2 * (zl % 2)) * 2 + k}

    def xpeer(o):
        return {"ctx": lax.rem(c + o, NX), "tp": t, "dp": d}

    def ypeer(o):
        return {"ctx": c, "tp": 2 * lax.rem(y + o, NY) + h, "dp": d}

    def rcopy(src, dst, ss, rs, dev):
        return pltpu.make_async_remote_copy(
            src_ref=src, dst_ref=dst, send_sem=ss, recv_sem=rs, device_id=dev, device_id_type=MESH
        )

    sent = []

    def go(copy):
        copy.start()
        sent.append(copy)

    barrier = pltpu.get_barrier_semaphore()
    peers = [pair, sib, across, inner] + [xpeer(o) for o in (1, 2, 3)] + [ypeer(o) for o in (1, 3)]
    for dev in peers:
        pl.semaphore_signal(barrier, inc=1, device_id=dev, device_id_type=MESH)
    pl.semaphore_wait(barrier, len(peers))

    kv_pair = rcopy(kv_ref, kvbuf.at[c, :, h], s_kv.at[0], r_kvz, pair)
    kv_pair.start()

    def kv_own(o):
        return rcopy(kv_ref, kvbuf.at[c, :, h], s_kv.at[o], r_kvx.at[o - 1, 0], xpeer(o))

    def kv_fwd(o):
        return rcopy(
            kvbuf.at[c, :, hp], kvbuf.at[c, :, hp], s_kv.at[3 + o], r_kvx.at[o - 1, 1], xpeer(o)
        )

    for o in (1, 2, 3):
        pl.when(c + o < NX)(lambda o=o: kv_own(o).start())
    kv_loc = pltpu.make_async_copy(kv_ref, kvbuf.at[c, :, h], loc.at[0])
    kv_loc.start()
    q_loc = pltpu.make_async_copy(q_ref.at[:, h], qown, loc.at[1])
    q_loc.start()
    w_loc = pltpu.make_async_copy(w_ref, wbuf.at[h, c], loc.at[2])
    w_loc.start()
    ein_loc = pltpu.make_async_copy(ein_ref, einbuf.at[:, h], loc.at[3])
    ein_loc.start()
    ed_loc = pltpu.make_async_copy(ed_ref, edbuf.at[h], loc.at[4])
    ed_loc.start()

    w_across = rcopy(w_ref.at[k], wbuf.at[h, c, k], s_w.at[0], r_wz, across)
    w_inner = rcopy(wbuf.at[hp, c, k], wbuf.at[hp, c, k], s_w.at[14], r_wz, inner)

    @pl.when(edge)
    def _():
        w_across.start()

    vext[:, :, HD:] = jnp.ones((NX, 1024, HD), BF)

    def spread_q(src, which):
        for b in range(4):
            block = src[b]
            for j in range(4):
                q2[which, j, b] = block[:, j * HD : (j + 1) * HD]

    q_loc.wait()
    spread_q(qown, h)

    q_pair = rcopy(q_ref.at[:, hp], qother, s_q, r_q, pair)
    kv_loc.wait()
    kv_pair.wait_recv()
    q_pair.start()
    for o in (1, 2, 3):
        pl.when(c + o < NX)(lambda o=o: kv_fwd(o).start())

    def put_v(src):
        vext[src, :, :HD] = kvbuf[src, 1].reshape(HD, 1024).astype(F32).T.astype(BF)

    put_v(c)
    def w_own(o):
        return rcopy(w_ref.at[k], wbuf.at[h, c, k], s_w.at[o], r_wx.at[o - 1, 0], xpeer(o))

    def w_fwd(o):
        return rcopy(
            wbuf.at[hp, c, k], wbuf.at[hp, c, k], s_w.at[3 + o], r_wx.at[o - 1, 1], xpeer(o)
        )

    w_sib = rcopy(wbuf.at[hp, c, k], wbuf.at[hp, c, k], s_w.at[7], r_ws.at[0], sib)

    def w_sib_own(o):
        cs = lax.rem(c + NX - o, NX)
        return rcopy(wbuf.at[h, cs, k], wbuf.at[h, cs, k], s_w.at[7 + o], r_ws.at[o], sib)

    def w_sib_fwd(o):
        cs = lax.rem(c + NX - o, NX)
        return rcopy(wbuf.at[hp, cs, k], wbuf.at[hp, cs, k], s_w.at[10 + o], r_ws.at[3 + o], sib)

    def e_part(ref_in, ref_down, j, side):
        if j < 4:
            return ref_in.at[k, j] if side is None else ref_in.at[k, side, j]
        return ref_down.at[k, j - 4] if side is None else ref_down.at[side, k, j - 4]

    def e_across(j):
        return rcopy(
            e_part(ein_ref, ed_ref, j, None), e_part(einbuf, edbuf, j, h),
            s_e.at[0, j], r_e.at[j], across,
        )

    def e_inner(j):
        part = e_part(einbuf, edbuf, j, hp)
        return rcopy(part, part, s_e.at[1, j], r_e.at[j], inner)

    def e_pass(j):
        @pl.when(edge)
        def _():
            e_across(j).wait_recv()
            e_inner(j).start()

    ein_sib = rcopy(einbuf.at[k, hp], einbuf.at[k, hp], s_sib.at[0], r_sib.at[0], sib)
    ed_sib = rcopy(edbuf.at[hp, k], edbuf.at[hp, k], s_sib.at[1], r_sib.at[1], sib)

    row_at = lax.broadcasted_iota(jnp.int32, (4, ROWS, 256), 1).reshape(4 * ROWS, 256) + h * ROWS
    col_at = lax.broadcasted_iota(jnp.int32, (4 * ROWS, 256), 1)
    allowed = col_at <= row_at

    def diagonal(which):
        keys = kvbuf[c, 0].reshape(HD, 1024)
        for b in range(4):
            kl = (b + 1) * 256
            qs = q2[which, :, b].reshape(4 * ROWS, HD)
            s = jnp.dot(qs, keys[:, :kl], preferred_element_type=F32)
            last = jnp.where(allowed, s[:, kl - 256 :], -1e30)
            s = last if b == 0 else jnp.concatenate([s[:, : kl - 256], last], axis=1)
            top = jnp.broadcast_to(jnp.max(s, axis=1, keepdims=True) * SCALE2, (4 * ROWS, HD))
            p = jnp.exp2(s * SCALE2 - jnp.concatenate([top] * (kl // HD), axis=1)).astype(BF)
            acc[which, :, b] = jnp.dot(
                p, vext[c, :kl], preferred_element_type=F32
            ).reshape(4, ROWS, 2 * HD)
            mrow[which, :, b] = top.reshape(4, ROWS, HD)

    def full_block(which, src):
        keys = kvbuf[src, 0].reshape(HD, 1024)
        for j in range(4):
            qs = q2[which, j].reshape(4 * ROWS, HD)
            s = jnp.dot(qs, keys, preferred_element_type=F32)
            old = mrow[which, j].reshape(4 * ROWS, HD)
            top = jnp.maximum(old, jnp.max(s, axis=1, keepdims=True) * SCALE2)
            factor = jnp.exp2(old - top)
            p = jnp.exp2(s * SCALE2 - jnp.concatenate([top] * 8, axis=1)).astype(BF)
            update = jnp.dot(p, vext[src], preferred_element_type=F32)
            acc[which, j] = (
                acc[which, j].reshape(4 * ROWS, 2 * HD) * jnp.concatenate([factor] * 2, axis=1)
                + update
            ).reshape(4, ROWS, 2 * HD)
            mrow[which, j] = top.reshape(4, ROWS, HD)

    def group(g, carry):
        which = lax.rem(h + g, 2)

        @pl.when(g == 1)
        def _():
            q_pair.wait_recv()
            @pl.when(jnp.logical_not(edge))
            def _():
                w_across.wait_recv()

            for o in (1, 3, 2):
                w_fwd(o).start()
            w_sib.start()

            @pl.when(edge)
            def _():
                for j in range(6):
                    e_across(j).start()

            spread_q(qother, hp)

        diagonal(which)

        @pl.when(g == 0)
        def _():
            for o in (1, 3, 2):
                w_own(o).start()

            @pl.when(edge)
            def _():
                w_across.wait_recv()
                w_inner.start()

        def earlier(o, carry):
            src = c - o

            @pl.when(g == 0)
            def _():
                rcopy(
                    kv_ref, kvbuf.at[src, :, h], s_kv.at[o], r_kvx.at[o - 1, 0], xpeer(o)
                ).wait_recv()
                rcopy(
                    kv_ref, kvbuf.at[src, :, hp], s_kv.at[o], r_kvx.at[o - 1, 1], xpeer(o)
                ).wait_recv()
                put_v(src)

            full_block(which, src)
            return carry

        lax.fori_loop(1, c + 1, earlier, 0)
        return carry

    lax.fori_loop(0, 2, group, 0)

    for w in range(2):
        for j in range(4):
            whole = acc[w, j].reshape(4 * ROWS, 2 * HD)
            head = (whole[:, :HD] / whole[:, HD:]).astype(BF)
            att[:, :, (4 * w + j) * HD : (4 * w + j + 1) * HD] = head.reshape(4, ROWS, HD)

    e_pass(0)
    for o in (1, 3, 2):
        w_own(o).wait_recv()
        w_sib_own(o).start()
    w_loc.wait()
    w_sib.wait_recv()

    def op_copy(i, side):
        return rcopy(
            sbuf.at[i, lax.rem(y + 2, NY), :, pl.ds(512 * side, 512)], oph.at[side, i],
            s_op.at[side, i], r_op.at[side, i], ypeer(1 + 2 * side),
        )

    def nb_copy(i, side):
        return rcopy(
            sbuf.at[i, lax.rem(y + 1 + 2 * side, NY)], rsbuf.at[side, i],
            s_rs.at[side, i], r_rs.at[side, i], ypeer(1 + 2 * side),
        )

    order = (0, 1, 3, 2)
    for i, o in enumerate(order):
        cs = lax.rem(c + NX - o, NX)
        if o:
            w_fwd(o).wait_recv()
            w_sib_fwd(o).start()
            w_sib_own(o).wait_recv()
            w_sib_fwd(o).wait_recv()

        def tile(n, carry, cs=cs, i=i):
            at = pl.ds(pl.multiple_of(n * 256, 256), 256)
            rows = att[...].reshape(4 * ROWS, 1024)
            w0 = jnp.concatenate([wbuf[0, cs, 0, :, at], wbuf[0, cs, 1, :, at]], axis=0)
            w1 = jnp.concatenate([wbuf[1, cs, 0, :, at], wbuf[1, cs, 1, :, at]], axis=0)
            part = jnp.dot(rows[:, :512], w0, preferred_element_type=F32)
            part = part + jnp.dot(rows[:, 512:], w1, preferred_element_type=F32)
            sbuf[i, :, :, at] = part.astype(BF).reshape(4, ROWS, 256)
            return carry

        lax.fori_loop(0, 4, tile, 0)
        for side in range(2):
            go(op_copy(i, side))
    for i in range(4):
        for side in range(2):
            op_copy(i, side).wait_recv()
            to = lax.rem(y + 1 + 2 * side, NY)
            lo = 512 * side
            sbuf[i, to, :, lo : lo + 512] = (
                sbuf[i, to, :, lo : lo + 512].astype(F32) + oph[side, i].astype(F32)
            ).astype(BF)
            go(nb_copy(i, side))
    e_pass(1)

    slot_at = lax.broadcasted_iota(jnp.int32, (ROWS, ROWS), 0)
    lane_at = lax.broadcasted_iota(jnp.int32, (ROWS, ROWS), 1)
    group_at = sum((slot_at >= n * CAP).astype(jnp.int32) for n in (1, 2, 3, 4))
    expert_at = group_at + c
    expert_at = jnp.where(expert_at >= NX, expert_at - NX, expert_at)
    expert_at = jnp.where(group_at == 4, -1, expert_at)
    match = jnp.zeros((ROWS, ROWS), F32)
    gate = jnp.zeros((ROWS, ROWS), F32)
    for n in range(8):
        hit = ids_ref[n : n + 1, :] == expert_at
        match = match + jnp.where(hit, 1.0, 0.0)
        gate = gate + jnp.where(hit, gw_ref[n : n + 1, :], 0.0)
    before = jnp.where(slot_at < lane_at, 1.0, 0.0).astype(BF)
    rank = jnp.dot(match.astype(BF), before, preferred_element_type=F32)
    want = (slot_at - group_at * CAP).astype(F32)
    chosen = jnp.where(rank == want, match, 0.0)
    weighted = (chosen * gate).T
    chosen = chosen.astype(BF)

    square = jnp.zeros((ROWS, 1), F32)
    for i, o in enumerate(order):
        cs = lax.rem(c + NX - o, NX)
        at = pl.ds(pl.multiple_of(cs * 1024, 1024), 1024)
        for side in range(2):
            nb_copy(i, side).wait_recv()
        total = sbuf[i, y].astype(F32) + rsbuf[0, i].astype(F32) + rsbuf[1, i].astype(F32)
        block = (res_ref[:, at].astype(F32) + total).astype(BF)
        stream[:, at] = block
        wide = block.astype(F32)
        square = square + jnp.sum(wide * wide, axis=1, keepdims=True)
        if i in (1, 2):
            e_pass(1 + i)
    inv = lax.rsqrt(square * (1.0 / D) + 1e-6)

    def x_copy(half, o):
        return rcopy(
            packed.at[o, half], xd.at[o - 1, half], s_x.at[half, o - 1], r_x.at[half, o - 1], xpeer(o)
        )

    def y_copy(half, side):
        return rcopy(
            disp.at[half, 0], disp.at[half, 1 + 2 * side], s_y.at[half, side], r_y.at[half, side],
            ypeer(1 + 2 * side),
        )

    def y_pass(half):
        return rcopy(
            disp.at[half, 1 + 2 * half], disp.at[half, 2], s_yp.at[half], r_yp.at[half],
            ypeer(1 + 2 * half),
        )

    def merge(pieces, quarter, extra):
        lo = (quarter % 2) * CAP
        return jnp.concatenate([p[lo : lo + CAP] for p in pieces] + extra, axis=0).astype(BF)

    def split(rows, quarter):
        lo = (quarter % 2) * CAP
        for o in range(NX):
            xsend[o, lo : lo + CAP] = rows[o * CAP : (o + 1) * CAP]

    for half in range(2):
        for quarter in (2 * half, 2 * half + 1):
            at = slice(quarter * 1024, (quarter + 1) * 1024)
            normed = (stream[:, at].astype(F32) * inv * gain_ref[:, at]).astype(BF)
            split(jnp.dot(chosen, normed, preferred_element_type=F32), quarter)
        packed[:, half] = xsend[...].astype(BF)
        for o in (2, 1, 3):
            go(x_copy(half, o))
    e_pass(4)
    for half in range(2):
        for o in (1, 3, 2):
            x_copy(half, o).wait_recv()
        pieces = [packed[0, half].astype(F32)] + [xd[o, half].astype(F32) for o in range(3)]
        for n in range(2):
            disp[half, 0, :, n * 1024 : (n + 1) * 1024] = merge(pieces, n, [])
        for side in range(2):
            go(y_copy(half, side))
    e_pass(5)

    @pl.when(jnp.logical_not(edge))
    def _():
        for j in range(6):
            e_inner(j).wait_recv()

    go(ein_sib)
    go(ed_sib)
    y_copy(0, 0).wait_recv()
    go(y_pass(0))
    y_copy(1, 1).wait_recv()
    go(y_pass(1))
    ein_loc.wait()
    ed_loc.wait()
    ein_sib.wait_recv()
    ed_sib.wait_recv()
    y_copy(0, 1).wait_recv()
    y_copy(1, 0).wait_recv()
    y_pass(0).wait_recv()
    y_pass(1).wait_recv()

    def project_in(n):
        total = jnp.zeros((4 * EROWS, 384), F32)
        for kk in range(4):
            lo = (kk % 2) * 1024
            total = total + lax.dot_general(
                disp[kk // 2, :, :, lo : lo + 1024].reshape(4 * EROWS, 1024),
                einbuf[n, :, :, :, kk * 1024 : (kk + 1) * 1024].reshape(384, 1024),
                NT,
                preferred_element_type=F32,
            )
        return total

    gate_part = project_in(0)
    hidden = (gate_part / (1.0 + jnp.exp(-gate_part)) * project_in(1)).astype(BF)

    def ro_copy(half):
        return rcopy(
            down.at[half, 2], rop.at[half], s_ro.at[half], r_ro.at[half], ypeer(1 + 2 * half)
        )

    def rn_copy(half, side):
        return rcopy(
            down.at[half, 3 - 2 * side], rnb.at[half, side], s_rn.at[half, side],
            r_rn.at[half, side], ypeer(1 + 2 * side),
        )

    for half in range(2):

        def down_tile(n, carry, half=half):
            lo = pl.multiple_of(n * 512, 512)
            weights = edbuf[:, :, :, :, pl.ds(half * HALF + lo, 512)].reshape(384, 512)
            part = jnp.dot(hidden, weights, preferred_element_type=F32)
            down[half, :, :, pl.ds(lo, 512)] = part.astype(BF).reshape(4, EROWS, 512)
            return carry

        lax.fori_loop(0, HALF // 512, down_tile, 0)
        if half == 0:
            go(ro_copy(0))
            go(rn_copy(0, 1))
        else:
            go(ro_copy(1))
    for half in range(2):
        ro_copy(half).wait_recv()
        slot = 3 - 2 * half
        down[half, slot] = (down[half, slot].astype(F32) + rop[half].astype(F32)).astype(BF)
        go(rn_copy(half, half))
        if half == 0:
            go(rn_copy(1, 0))

    def rx_copy(half, o):
        return rcopy(
            back.at[o, half], eb.at[o - 1, half], s_rx.at[half, o - 1], r_rx.at[half, o - 1],
            xpeer(NX - o),
        )

    for half in range(2):
        for side in range(2):
            rn_copy(half, side).wait_recv()
        for n in range(2):
            at = slice(n * 1024, (n + 1) * 1024)
            total = down[half, 0, :, at].astype(F32)
            for side in range(2):
                total = total + rnb[half, side, :, at].astype(F32)
            split(total, n)
        back[:, half] = xsend[...].astype(BF)
        for o in (2, 1, 3):
            go(rx_copy(half, o))
    high = weighted.astype(BF)
    rest = weighted - high.astype(F32)
    mid = rest.astype(BF)
    low = (rest - mid.astype(F32)).astype(BF)
    for half in range(2):
        for o in (1, 3, 2):
            rx_copy(half, o).wait_recv()
        pieces = [back[0, half].astype(F32)] + [eb[o, half].astype(F32) for o in range(3)]
        for n in range(2):
            at = slice(half * HALF + n * 1024, half * HALF + (n + 1) * 1024)
            rows = merge(pieces, n, [jnp.zeros((ROWS - EROWS, 1024), F32)])
            added = (
                jnp.dot(high, rows, preferred_element_type=F32)
                + jnp.dot(mid, rows, preferred_element_type=F32)
                + jnp.dot(low, rows, preferred_element_type=F32)
            )
            out_ref[:, at] = (stream[:, at].astype(F32) + added).astype(BF)

    kv_pair.wait_send()
    for o in (1, 2, 3):

        @pl.when(c + o < NX)
        def _(o=o):
            kv_own(o).wait_send()
            kv_fwd(o).wait_send()

    q_pair.wait_send()
    w_sib.wait_send()
    for o in (1, 2, 3):
        w_own(o).wait_send()
        w_fwd(o).wait_send()
        w_sib_own(o).wait_send()
        w_sib_fwd(o).wait_send()

    @pl.when(edge)
    def _():
        w_across.wait_send()
        w_inner.wait_send()
        for j in range(6):
            e_across(j).wait_send()
            e_inner(j).wait_send()

    for copy in sent:
        copy.wait_send()


def body(residual, queries, key_value, out_proj, norm_gain, expert_ids, gate_weights, expert_in, expert_down):
    sem = pltpu.SemaphoreType.DMA
    vmem = pl.BlockSpec(memory_space=pltpu.VMEM)
    hbm = pl.BlockSpec(memory_space=pl.ANY)
    scratch = [
        pltpu.VMEM((NX, 2, 2, 64, 1024), BF),
        pltpu.VMEM((NX, 1024, 2 * HD), BF),
        pltpu.VMEM((2, 4, 4, ROWS, HD), BF),
        pltpu.VMEM((4, ROWS, 512), BF),
        pltpu.VMEM((4, ROWS, 512), BF),
        pltpu.VMEM((2, 4, 4, ROWS, 2 * HD), F32),
        pltpu.VMEM((2, 4, 4, ROWS, HD), F32),
        pltpu.VMEM((4, ROWS, 1024), BF),
        pltpu.VMEM((2, NX, 2, 256, 1024), BF),
        pltpu.VMEM((4, NY, ROWS, 1024), BF),
        pltpu.VMEM((2, 4, ROWS, 512), BF),
        pltpu.VMEM((2, 4, ROWS, 1024), BF),
        pltpu.VMEM((ROWS, D), BF),
        pltpu.VMEM((NX, 2 * CAP, 1024), F32),
        pltpu.VMEM((NX, 2, 2 * CAP, 1024), BF),
        pltpu.VMEM((3, 2, 2 * CAP, 1024), BF),
        pltpu.VMEM((2, NY, EROWS, HALF), BF),
        pltpu.VMEM((2, NY, EROWS, HALF), BF),
        pltpu.VMEM((2, EROWS, HALF), BF),
        pltpu.VMEM((2, 2, EROWS, HALF), BF),
        pltpu.VMEM((NX, 2, 2 * CAP, 1024), BF),
        pltpu.VMEM((3, 2, 2 * CAP, 1024), BF),
        pltpu.VMEM((2, 2, 4, 48, D), BF),
        pltpu.VMEM((2, 2, 2, 48, D), BF),
        sem((5,)),
        sem((7,)), sem, sem((3, 2)),
        sem, sem,
        sem((15,)), sem, sem((3, 2)), sem((7,)),
        sem((2, 4)), sem((2, 4)), sem((2, 4)), sem((2, 4)),
        sem((2, 6)), sem((6,)), sem((2,)), sem((2,)),
        sem((2, 3)), sem((2, 3)), sem((2, 2)), sem((2, 2)), sem((2,)), sem((2,)),
        sem((2,)), sem((2,)), sem((2, 2)), sem((2, 2)), sem((2, 3)), sem((2, 3)),
    ]
    return pl.pallas_call(
        kernel,
        out_shape=jax.ShapeDtypeStruct((ROWS, D), BF),
        in_specs=[hbm, hbm, hbm, vmem, vmem, vmem, vmem, hbm, hbm],
        out_specs=vmem,
        scratch_shapes=scratch,
        compiler_params=pltpu.CompilerParams(
            collective_id=0, has_side_effects=True, vmem_limit_bytes=62 * 1024 * 1024
        ),
        name="layer",
    )(
        queries.reshape(4, 2, ROWS, 512),
        jnp.swapaxes(key_value, 1, 2),
        out_proj.reshape(2, 256, 1024),
        residual,
        norm_gain.reshape(1, D),
        expert_ids.T,
        gate_weights.T,
        jnp.swapaxes(expert_in[0], 1, 2).reshape(2, 4, 48, D),
        expert_down[0].reshape(2, 2, 48, D),
    )


def solution(mesh):
    in_specs = (
        P(("dp", "ctx", "tp"), None),
        P(("dp", "ctx"), "tp"),
        P(None, ("dp", "ctx"), "tp"),
        P("tp", "ctx"),
        P(),
        P(("dp", "ctx", "tp"), None),
        P(("dp", "ctx", "tp"), None),
        P("ctx", None, None, "tp"),
        P("ctx", "tp", None),
    )
    out_specs = P(("dp", "ctx", "tp"), None)
    return jax.shard_map(body, mesh=mesh, in_specs=in_specs, out_specs=out_specs, check_vma=False)
```

```python
import jax
import jax.numpy as jnp
from jax import lax
from jax.experimental import pallas as pl
from jax.experimental.pallas import tpu as pltpu
from jax.sharding import PartitionSpec as P

HD = 128
CAP = 24
D = 4096
HALF = D // 2
NX = 4
NY = 4
ROWS = 128
EROWS = NX * CAP
MESH = pl.DeviceIdType.MESH
BF = jnp.bfloat16
F32 = jnp.float32
SCALE2 = HD ** (-0.5) * 1.4426950408889634
NT = (((1,), (1,)), ((), ()))


def kernel(
    q_ref, kv_ref, w_ref, res_ref, gain_ref, ids_ref, gw_ref, ein_ref, ed_ref,
    out_ref,
    kvbuf, vext, q2, qown, qother, acc, mrow, att, wbuf, sbuf, oph, rsbuf, stream,
    xsend, packed, xd, disp, down, rop, rnb, back, eb, einbuf, edbuf,
    loc, s_kv, r_kvz, r_kvx, s_q, r_q, s_w, r_wz, r_wx, s_wo, r_wo, r_ws,
    s_op, r_op, s_rs, r_rs, s_e, r_e, s_sib, r_sib, s_x, r_x, s_y, r_y, s_yp, r_yp,
    s_ro, r_ro, s_rn, r_rn, s_rx, r_rx,
):
    c = lax.axis_index("ctx")
    t = lax.axis_index("tp")
    d = lax.axis_index("dp")
    y = t // 2
    h = t % 2
    k = d % 2
    hp = 1 - h
    kp = 1 - k

    zl = d // 2
    edge = (zl == 0) | (zl == 3)
    pair = {"ctx": c, "tp": 2 * y + hp, "dp": d}
    sib = {"ctx": c, "tp": t, "dp": d + 1 - 2 * k}
    near = {"ctx": c, "tp": t, "dp": (zl + 1 - 2 * (zl % 2)) * 2 + k}
    far = {"ctx": c, "tp": 2 * y + jnp.where(edge, hp, h), "dp": (3 - zl) * 2 + k}

    def xpeer(o):
        return {"ctx": lax.rem(c + o, NX), "tp": t, "dp": d}

    def ypeer(o):
        return {"ctx": c, "tp": 2 * lax.rem(y + o, NY) + h, "dp": d}

    def rcopy(src, dst, ss, rs, dev):
        return pltpu.make_async_remote_copy(
            src_ref=src, dst_ref=dst, send_sem=ss, recv_sem=rs, device_id=dev, device_id_type=MESH
        )

    sent = []

    def go(copy):
        copy.start()
        sent.append(copy)

    barrier = pltpu.get_barrier_semaphore()
    peers = [pair, sib, near, far] + [xpeer(o) for o in (1, 2, 3)] + [ypeer(o) for o in (1, 3)]
    for dev in peers:
        pl.semaphore_signal(barrier, inc=1, device_id=dev, device_id_type=MESH)
    pl.semaphore_wait(barrier, len(peers))

    kv_pair = rcopy(kv_ref, kvbuf.at[c, :, h], s_kv.at[0], r_kvz, pair)
    kv_pair.start()

    def kv_own(o):
        return rcopy(kv_ref, kvbuf.at[c, :, h], s_kv.at[o], r_kvx.at[o - 1, 0], xpeer(o))

    def kv_fwd(o):
        return rcopy(
            kvbuf.at[c, :, hp], kvbuf.at[c, :, hp], s_kv.at[3 + o], r_kvx.at[o - 1, 1], xpeer(o)
        )

    for o in (1, 2, 3):
        pl.when(c + o < NX)(lambda o=o: kv_own(o).start())
    kv_loc = pltpu.make_async_copy(kv_ref, kvbuf.at[c, :, h], loc.at[0])
    kv_loc.start()
    q_loc = pltpu.make_async_copy(q_ref.at[:, h], qown, loc.at[1])
    q_loc.start()
    w_loc = pltpu.make_async_copy(w_ref, wbuf.at[h, c], loc.at[2])
    w_loc.start()
    ein_loc = pltpu.make_async_copy(ein_ref, einbuf.at[:, h], loc.at[3])
    ein_loc.start()
    ed_loc = pltpu.make_async_copy(ed_ref, edbuf.at[h], loc.at[4])
    ed_loc.start()

    w_pair = rcopy(w_ref.at[k], wbuf.at[h, c, k], s_w.at[0], r_wz, pair)

    vext[:, :, HD:] = jnp.ones((NX, 1024, HD), BF)

    def spread_q(src, which, heads):
        for b in range(4):
            block = src[b]
            for n, j in enumerate(heads):
                q2[which, j, b] = block[:, n * HD : (n + 1) * HD]

    q_loc.wait()
    spread_q(qown, h, range(4))

    def q_pair(n):
        return rcopy(
            q_ref.at[:, hp, :, pl.ds(256 * n, 256)], qother.at[n], s_q.at[n], r_q.at[n], pair
        )

    kv_loc.wait()
    kv_pair.wait_recv()
    for o in (1, 2, 3):
        pl.when(c + o < NX)(lambda o=o: kv_fwd(o).start())
    go(q_pair(0))
    go(w_pair)
    go(q_pair(1))

    def put_v(src):
        vext[src, :, :HD] = kvbuf[src, 1].reshape(HD, 1024).astype(F32).T.astype(BF)

    put_v(c)
    def w_own(o):
        return rcopy(w_ref.at[k], wbuf.at[h, c, k], s_w.at[o], r_wx.at[o // 2, 0], xpeer(o))

    def w_fwd(o):
        part = wbuf.at[hp, c, k]
        return rcopy(part, part, s_w.at[3 + o], r_wx.at[o // 2, 1], xpeer(o))

    def w_opp(side, which):
        part = wbuf.at[hp if which else h, lax.rem(c + 3 - 2 * side, NX), k, side]
        return rcopy(
            part, part, s_wo.at[side, which], r_wo.at[side, which], xpeer(1 + 2 * side)
        )

    w_sib = rcopy(wbuf.at[hp, c, k], wbuf.at[hp, c, k], s_w.at[7], r_ws.at[0], sib)

    def w_sib_own(o):
        cs = lax.rem(c + NX - o, NX)
        return rcopy(wbuf.at[h, cs, k], wbuf.at[h, cs, k], s_w.at[7 + o], r_ws.at[o], sib)

    def w_sib_fwd(o):
        cs = lax.rem(c + NX - o, NX)
        return rcopy(wbuf.at[hp, cs, k], wbuf.at[hp, cs, k], s_w.at[10 + o], r_ws.at[3 + o], sib)

    def e_part(ref_in, ref_down, j, side):
        if j < 4:
            return ref_in.at[k, j] if side is None else ref_in.at[k, side, j]
        return ref_down.at[k, j - 4] if side is None else ref_down.at[side, k, j - 4]

    def e_across(j):
        return rcopy(
            e_part(ein_ref, ed_ref, j, None), e_part(einbuf, edbuf, j, h),
            s_e.at[0, j], r_e.at[j], far,
        )

    def e_inner(j):
        part = e_part(einbuf, edbuf, j, hp)
        return rcopy(part, part, s_e.at[1, j], r_e.at[j], near)

    def e_pass(j):
        @pl.when(edge)
        def _():
            e_across(j).wait_recv()
            e_inner(j).start()

    ein_sib = rcopy(einbuf.at[k, hp], einbuf.at[k, hp], s_sib.at[0], r_sib.at[0], sib)
    ed_sib = rcopy(edbuf.at[hp, k], edbuf.at[hp, k], s_sib.at[1], r_sib.at[1], sib)

    row_at = lax.broadcasted_iota(jnp.int32, (2, ROWS, 256), 1).reshape(2 * ROWS, 256) + h * ROWS
    col_at = lax.broadcasted_iota(jnp.int32, (2 * ROWS, 256), 1)
    allowed = col_at <= row_at

    def diagonal(which, j0):
        keys = kvbuf[c, 0].reshape(HD, 1024)
        for b in range(4):
            kl = (b + 1) * 256
            qs = q2[which, pl.ds(j0, 2), b].reshape(2 * ROWS, HD)
            s = jnp.dot(qs, keys[:, :kl], preferred_element_type=F32)
            last = jnp.where(allowed, s[:, kl - 256 :], -1e30)
            s = last if b == 0 else jnp.concatenate([s[:, : kl - 256], last], axis=1)
            top = jnp.broadcast_to(jnp.max(s, axis=1, keepdims=True) * SCALE2, (2 * ROWS, HD))
            p = jnp.exp2(s * SCALE2 - jnp.concatenate([top] * (kl // HD), axis=1)).astype(BF)
            acc[which, pl.ds(j0, 2), b] = jnp.dot(
                p, vext[c, :kl], preferred_element_type=F32
            ).reshape(2, ROWS, 2 * HD)
            mrow[which, pl.ds(j0, 2), b] = top.reshape(2, ROWS, HD)

    def full_block(which, j0, src):
        keys = kvbuf[src, 0].reshape(HD, 1024)
        for n in range(2):
            j = j0 + n
            qs = q2[which, j].reshape(4 * ROWS, HD)
            s = jnp.dot(qs, keys, preferred_element_type=F32)
            old = mrow[which, j].reshape(4 * ROWS, HD)
            top = jnp.maximum(old, jnp.max(s, axis=1, keepdims=True) * SCALE2)
            factor = jnp.exp2(old - top)
            p = jnp.exp2(s * SCALE2 - jnp.concatenate([top] * 8, axis=1)).astype(BF)
            update = jnp.dot(p, vext[src], preferred_element_type=F32)
            acc[which, j] = (
                acc[which, j].reshape(4 * ROWS, 2 * HD) * jnp.concatenate([factor] * 2, axis=1)
                + update
            ).reshape(4, ROWS, 2 * HD)
            mrow[which, j] = top.reshape(4, ROWS, HD)

    def group(g, carry):
        which = lax.rem(h + g // 2, 2)
        j0 = 2 * (g % 2)

        @pl.when(g == 2)
        def _():
            q_pair(0).wait_recv()
            spread_q(qother.at[0], hp, (0, 1))

        @pl.when(g == 3)
        def _():
            w_pair.wait_recv()
            for o in (1, 3):
                w_fwd(o).start()
            w_sib.start()
            q_pair(1).wait_recv()
            spread_q(qother.at[1], hp, (2, 3))

            @pl.when(edge)
            def _():
                for j in range(6):
                    e_across(j).start()

        diagonal(which, j0)

        def earlier(o, carry):
            src = c - o

            @pl.when(g == 0)
            def _():
                rcopy(
                    kv_ref, kvbuf.at[src, :, h], s_kv.at[o], r_kvx.at[o - 1, 0], xpeer(o)
                ).wait_recv()
                rcopy(
                    kv_ref, kvbuf.at[src, :, hp], s_kv.at[o], r_kvx.at[o - 1, 1], xpeer(o)
                ).wait_recv()
                put_v(src)

            full_block(which, j0, src)
            return carry

        lax.fori_loop(1, c + 1, earlier, 0)

        @pl.when(g == 0)
        def _():
            for o in (1, 2, 3):

                @pl.when(c + o < NX)
                def _(o=o):
                    kv_own(o).wait_send()
                    kv_fwd(o).wait_send()

            for o in (1, 3):
                w_own(o).start()

        return carry

    lax.fori_loop(0, 4, group, 0)

    for w in range(2):
        for j in range(4):
            whole = acc[w, j].reshape(4 * ROWS, 2 * HD)
            head = (whole[:, :HD] / whole[:, HD:]).astype(BF)
            att[:, :, (4 * w + j) * HD : (4 * w + j + 1) * HD] = head.reshape(4, ROWS, HD)

    for o in (1, 3):
        w_own(o).wait_recv()
        go(w_opp(o // 2, 0))
        w_sib_own(o).start()
    w_loc.wait()
    w_sib.wait_recv()

    def op_copy(i, side):
        return rcopy(
            sbuf.at[i, lax.rem(y + 2, NY), :, pl.ds(512 * side, 512)], oph.at[side, i],
            s_op.at[side, i], r_op.at[side, i], ypeer(1 + 2 * side),
        )

    def nb_copy(i, side):
        return rcopy(
            sbuf.at[i, lax.rem(y + 1 + 2 * side, NY)], rsbuf.at[side, i],
            s_rs.at[side, i], r_rs.at[side, i], ypeer(1 + 2 * side),
        )

    def add_own(i):
        for side in range(2):
            op_copy(i, side).wait_recv()
            to = lax.rem(y + 1 + 2 * side, NY)
            lo = 512 * side
            sbuf[i, to, :, lo : lo + 512] = (
                sbuf[i, to, :, lo : lo + 512].astype(F32) + oph[side, i].astype(F32)
            ).astype(BF)
            go(nb_copy(i, side))

    order = (0, 1, 3, 2)
    for i, o in enumerate(order):
        cs = lax.rem(c + NX - o, NX)
        if i == 1:
            for n in (1, 3):
                w_fwd(n).wait_recv()
                go(w_opp(n // 2, 1))
                w_sib_fwd(n).start()
        if i == 3:
            add_own(2)
            for which in range(2):
                for side in range(2):
                    w_opp(side, which).wait_recv()
            w_sib_own(o).start()
            w_sib_fwd(o).start()
        if i:
            w_sib_own(o).wait_recv()
            w_sib_fwd(o).wait_recv()

        def tile(n, carry, cs=cs, i=i):
            at = pl.ds(pl.multiple_of(n * 256, 256), 256)
            rows = att[...].reshape(4 * ROWS, 1024)
            w0 = wbuf[0, cs, :, :, :, at].reshape(512, 256)
            w1 = wbuf[1, cs, :, :, :, at].reshape(512, 256)
            part = jnp.dot(rows[:, :512], w0, preferred_element_type=F32)
            part = part + jnp.dot(rows[:, 512:], w1, preferred_element_type=F32)
            sbuf[i, :, :, at] = part.astype(BF).reshape(4, ROWS, 256)
            return carry

        lax.fori_loop(0, 4, tile, 0)
        for side in range(2):
            go(op_copy(i, side))
        if i in (1, 2):
            add_own(i - 1)
    add_own(3)
    e_pass(0)

    slot_at = lax.broadcasted_iota(jnp.int32, (ROWS, ROWS), 0)
    lane_at = lax.broadcasted_iota(jnp.int32, (ROWS, ROWS), 1)
    group_at = sum((slot_at >= n * CAP).astype(jnp.int32) for n in (1, 2, 3, 4))
    expert_at = group_at + c
    expert_at = jnp.where(expert_at >= NX, expert_at - NX, expert_at)
    expert_at = jnp.where(group_at == 4, -1, expert_at)
    match = jnp.zeros((ROWS, ROWS), F32)
    gate = jnp.zeros((ROWS, ROWS), F32)
    for n in range(8):
        hit = ids_ref[n : n + 1, :] == expert_at
        match = match + jnp.where(hit, 1.0, 0.0)
        gate = gate + jnp.where(hit, gw_ref[n : n + 1, :], 0.0)
    before = jnp.where(slot_at < lane_at, 1.0, 0.0).astype(BF)
    rank = jnp.dot(match.astype(BF), before, preferred_element_type=F32)
    want = (slot_at - group_at * CAP).astype(F32)
    chosen = jnp.where(rank == want, match, 0.0)
    weighted = (chosen * gate).T
    chosen = chosen.astype(BF)

    square = jnp.zeros((ROWS, 1), F32)
    for i, o in enumerate(order):
        cs = lax.rem(c + NX - o, NX)
        at = pl.ds(pl.multiple_of(cs * 1024, 1024), 1024)
        for side in range(2):
            nb_copy(i, side).wait_recv()
        total = sbuf[i, y].astype(F32) + rsbuf[0, i].astype(F32) + rsbuf[1, i].astype(F32)
        block = (res_ref[:, at].astype(F32) + total).astype(BF)
        stream[:, at] = block
        wide = block.astype(F32)
        square = square + jnp.sum(wide * wide, axis=1, keepdims=True)
        if i in (1, 3):
            e_pass(1 + i // 2)
    inv = lax.rsqrt(square * (1.0 / D) + 1e-6)

    def x_copy(half, o):
        return rcopy(
            packed.at[o, half], xd.at[o - 1, half], s_x.at[half, o - 1], r_x.at[half, o - 1], xpeer(o)
        )

    def y_copy(half, side):
        return rcopy(
            disp.at[half, 0], disp.at[half, 1 + 2 * side], s_y.at[half, side], r_y.at[half, side],
            ypeer(1 + 2 * side),
        )

    def y_pass(half):
        return rcopy(
            disp.at[half, 1 + 2 * half], disp.at[half, 2], s_yp.at[half], r_yp.at[half],
            ypeer(1 + 2 * half),
        )

    def merge(pieces, quarter, extra):
        lo = (quarter % 2) * CAP
        return jnp.concatenate([p[lo : lo + CAP] for p in pieces] + extra, axis=0).astype(BF)

    def split(rows, quarter):
        lo = (quarter % 2) * CAP
        for o in range(NX):
            xsend[o, lo : lo + CAP] = rows[o * CAP : (o + 1) * CAP]

    for half in range(2):
        for quarter in (2 * half, 2 * half + 1):
            at = slice(quarter * 1024, (quarter + 1) * 1024)
            normed = (stream[:, at].astype(F32) * inv * gain_ref[:, at]).astype(BF)
            split(jnp.dot(chosen, normed, preferred_element_type=F32), quarter)
        packed[:, half] = xsend[...].astype(BF)
        for o in (2, 1, 3):
            go(x_copy(half, o))
    e_pass(3)
    for half in range(2):
        for o in (1, 3, 2):
            x_copy(half, o).wait_recv()
        pieces = [packed[0, half].astype(F32)] + [xd[o, half].astype(F32) for o in range(3)]
        for n in range(2):
            disp[half, 0, :, n * 1024 : (n + 1) * 1024] = merge(pieces, n, [])
        for side in range(2):
            go(y_copy(half, side))
        e_pass(4 + half)

    @pl.when(jnp.logical_not(edge))
    def _():
        for j in range(6):
            e_inner(j).wait_recv()

    go(ein_sib)
    go(ed_sib)
    y_copy(0, 0).wait_recv()
    go(y_pass(0))
    y_copy(1, 1).wait_recv()
    go(y_pass(1))
    ein_loc.wait()
    ed_loc.wait()
    ein_sib.wait_recv()
    ed_sib.wait_recv()

    def project_in(n, half):
        total = jnp.zeros((4 * EROWS, 384), F32)
        for kk in range(2):
            lo = kk * 1024
            at = half * HALF + lo
            total = total + lax.dot_general(
                disp[half, :, :, lo : lo + 1024].reshape(4 * EROWS, 1024),
                einbuf[n, :, :, :, at : at + 1024].reshape(384, 1024),
                NT,
                preferred_element_type=F32,
            )
        return total

    y_copy(0, 1).wait_recv()
    y_pass(0).wait_recv()
    gate_part = project_in(0, 0)
    up_part = project_in(1, 0)
    y_copy(1, 0).wait_recv()
    y_pass(1).wait_recv()
    gate_part = gate_part + project_in(0, 1)
    up_part = up_part + project_in(1, 1)
    hidden = (gate_part / (1.0 + jnp.exp(-gate_part)) * up_part).astype(BF)

    def ro_copy(half):
        return rcopy(
            down.at[half, 2], rop.at[half], s_ro.at[half], r_ro.at[half], ypeer(1 + 2 * half)
        )

    def rn_copy(half, side):
        return rcopy(
            down.at[half, 3 - 2 * side], rnb.at[half, side], s_rn.at[half, side],
            r_rn.at[half, side], ypeer(1 + 2 * side),
        )

    for half in range(2):

        def down_tile(n, carry, half=half):
            lo = pl.multiple_of(n * 512, 512)
            weights = edbuf[:, :, :, :, pl.ds(half * HALF + lo, 512)].reshape(384, 512)
            part = jnp.dot(hidden, weights, preferred_element_type=F32)
            down[half, :, :, pl.ds(lo, 512)] = part.astype(BF).reshape(4, EROWS, 512)
            return carry

        lax.fori_loop(0, HALF // 512, down_tile, 0)
        if half == 0:
            go(ro_copy(0))
            go(rn_copy(0, 1))
        else:
            go(ro_copy(1))
    for half in range(2):
        ro_copy(half).wait_recv()
        slot = 3 - 2 * half
        down[half, slot] = (down[half, slot].astype(F32) + rop[half].astype(F32)).astype(BF)
        go(rn_copy(half, half))
        if half == 0:
            go(rn_copy(1, 0))

    def rx_copy(half, o):
        return rcopy(
            back.at[o, half], eb.at[o - 1, half], s_rx.at[half, o - 1], r_rx.at[half, o - 1],
            xpeer(NX - o),
        )

    for half in range(2):
        for side in range(2):
            rn_copy(half, side).wait_recv()
        for n in range(2):
            at = slice(n * 1024, (n + 1) * 1024)
            total = down[half, 0, :, at].astype(F32)
            for side in range(2):
                total = total + rnb[half, side, :, at].astype(F32)
            split(total, n)
        back[:, half] = xsend[...].astype(BF)
        for o in (2, 1, 3):
            go(rx_copy(half, o))
    high = weighted.astype(BF)
    rest = weighted - high.astype(F32)
    mid = rest.astype(BF)
    low = (rest - mid.astype(F32)).astype(BF)
    for half in range(2):
        for o in (1, 3, 2):
            rx_copy(half, o).wait_recv()
        pieces = [back[0, half].astype(F32)] + [eb[o, half].astype(F32) for o in range(3)]
        for n in range(2):
            at = slice(half * HALF + n * 1024, half * HALF + (n + 1) * 1024)
            rows = merge(pieces, n, [jnp.zeros((ROWS - EROWS, 1024), F32)])
            added = (
                jnp.dot(high, rows, preferred_element_type=F32)
                + jnp.dot(mid, rows, preferred_element_type=F32)
                + jnp.dot(low, rows, preferred_element_type=F32)
            )
            out_ref[:, at] = (stream[:, at].astype(F32) + added).astype(BF)

    kv_pair.wait_send()
    w_sib.wait_send()
    for o in (1, 2, 3):
        if o != 2:
            w_own(o).wait_send()
            w_fwd(o).wait_send()
        w_sib_own(o).wait_send()
        w_sib_fwd(o).wait_send()

    @pl.when(edge)
    def _():
        for j in range(6):
            e_across(j).wait_send()
            e_inner(j).wait_send()

    for copy in sent:
        copy.wait_send()


def body(residual, queries, key_value, out_proj, norm_gain, expert_ids, gate_weights, expert_in, expert_down):
    sem = pltpu.SemaphoreType.DMA
    vmem = pl.BlockSpec(memory_space=pltpu.VMEM)
    hbm = pl.BlockSpec(memory_space=pl.ANY)
    scratch = [
        pltpu.VMEM((NX, 2, 2, 64, 1024), BF),
        pltpu.VMEM((NX, 1024, 2 * HD), BF),
        pltpu.VMEM((2, 4, 4, ROWS, HD), BF),
        pltpu.VMEM((4, ROWS, 512), BF),
        pltpu.VMEM((2, 4, ROWS, 256), BF),
        pltpu.VMEM((2, 4, 4, ROWS, 2 * HD), F32),
        pltpu.VMEM((2, 4, 4, ROWS, HD), F32),
        pltpu.VMEM((4, ROWS, 1024), BF),
        pltpu.VMEM((2, NX, 2, 2, ROWS, 1024), BF),
        pltpu.VMEM((4, NY, ROWS, 1024), BF),
        pltpu.VMEM((2, 4, ROWS, 512), BF),
        pltpu.VMEM((2, 4, ROWS, 1024), BF),
        pltpu.VMEM((ROWS, D), BF),
        pltpu.VMEM((NX, 2 * CAP, 1024), F32),
        pltpu.VMEM((NX, 2, 2 * CAP, 1024), BF),
        pltpu.VMEM((3, 2, 2 * CAP, 1024), BF),
        pltpu.VMEM((2, NY, EROWS, HALF), BF),
        pltpu.VMEM((2, NY, EROWS, HALF), BF),
        pltpu.VMEM((2, EROWS, HALF), BF),
        pltpu.VMEM((2, 2, EROWS, HALF), BF),
        pltpu.VMEM((NX, 2, 2 * CAP, 1024), BF),
        pltpu.VMEM((3, 2, 2 * CAP, 1024), BF),
        pltpu.VMEM((2, 2, 4, 48, D), BF),
        pltpu.VMEM((2, 2, 2, 48, D), BF),
        sem((5,)),
        sem((7,)), sem, sem((3, 2)),
        sem((2,)), sem((2,)),
        sem((14,)), sem, sem((2, 2)), sem((2, 2)), sem((2, 2)), sem((7,)),
        sem((2, 4)), sem((2, 4)), sem((2, 4)), sem((2, 4)),
        sem((2, 6)), sem((6,)), sem((2,)), sem((2,)),
        sem((2, 3)), sem((2, 3)), sem((2, 2)), sem((2, 2)), sem((2,)), sem((2,)),
        sem((2,)), sem((2,)), sem((2, 2)), sem((2, 2)), sem((2, 3)), sem((2, 3)),
    ]
    return pl.pallas_call(
        kernel,
        out_shape=jax.ShapeDtypeStruct((ROWS, D), BF),
        in_specs=[hbm, hbm, hbm, vmem, vmem, vmem, vmem, hbm, hbm],
        out_specs=vmem,
        scratch_shapes=scratch,
        compiler_params=pltpu.CompilerParams(
            collective_id=0, has_side_effects=True, vmem_limit_bytes=62 * 1024 * 1024
        ),
        name="layer",
    )(
        queries.reshape(4, 2, ROWS, 512),
        jnp.swapaxes(key_value, 1, 2),
        out_proj.reshape(2, 2, ROWS, 1024),
        residual,
        norm_gain.reshape(1, D),
        expert_ids.T,
        gate_weights.T,
        jnp.swapaxes(expert_in[0], 1, 2).reshape(2, 4, 48, D),
        expert_down[0].reshape(2, 2, 48, D),
    )


def solution(mesh):
    in_specs = (
        P(("dp", "ctx", "tp"), None),
        P(("dp", "ctx"), "tp"),
        P(None, ("dp", "ctx"), "tp"),
        P("tp", "ctx"),
        P(),
        P(("dp", "ctx", "tp"), None),
        P(("dp", "ctx", "tp"), None),
        P("ctx", None, None, "tp"),
        P("ctx", "tp", None),
    )
    out_specs = P(("dp", "ctx", "tp"), None)
    return jax.shard_map(body, mesh=mesh, in_specs=in_specs, out_specs=out_specs, check_vma=False)
```

```python
import jax
import jax.numpy as jnp
from jax import lax
from jax.experimental import pallas as pl
from jax.experimental.pallas import tpu as pltpu
from jax.sharding import PartitionSpec as P

HD = 128
CAP = 24
D = 4096
HALF = D // 2
NX = 4
NY = 4
ROWS = 128
EROWS = NX * CAP
MESH = pl.DeviceIdType.MESH
BF = jnp.bfloat16
F32 = jnp.float32
SCALE2 = HD ** (-0.5) * 1.4426950408889634
NT = (((1,), (1,)), ((), ()))


def kernel(
    q_ref, kv_ref, w_ref, res_ref, gain_ref, ids_ref, gw_ref, ein_ref, ed_ref,
    out_ref,
    kvbuf, vext, q2, qown, qother, acc, mrow, att, wbuf, sbuf, oph, rsbuf, stream,
    xsend, packed, xd, disp, down, rop, rnb, back, eb, einbuf, edbuf,
    loc, s_kv, r_kvz, r_kvx, s_q, r_q, s_w, r_wz, r_wx, s_wo, r_wo, r_ws,
    s_op, r_op, s_rs, r_rs, s_e, r_e, s_sib, r_sib, s_x, r_x, s_y, r_y, s_yp, r_yp,
    s_ro, r_ro, s_rn, r_rn, s_rx, r_rx,
):
    c = lax.axis_index("ctx")
    t = lax.axis_index("tp")
    d = lax.axis_index("dp")
    y = t // 2
    h = t % 2
    k = d % 2
    hp = 1 - h
    kp = 1 - k

    zl = d // 2
    edge = (zl == 0) | (zl == 3)
    pair = {"ctx": c, "tp": 2 * y + hp, "dp": d}
    sib = {"ctx": c, "tp": t, "dp": d + 1 - 2 * k}
    near = {"ctx": c, "tp": t, "dp": (zl + 1 - 2 * (zl % 2)) * 2 + k}
    far = {"ctx": c, "tp": 2 * y + jnp.where(edge, hp, h), "dp": (3 - zl) * 2 + k}

    def xpeer(o):
        return {"ctx": lax.rem(c + o, NX), "tp": t, "dp": d}

    def ypeer(o):
        return {"ctx": c, "tp": 2 * lax.rem(y + o, NY) + h, "dp": d}

    def rcopy(src, dst, ss, rs, dev):
        return pltpu.make_async_remote_copy(
            src_ref=src, dst_ref=dst, send_sem=ss, recv_sem=rs, device_id=dev, device_id_type=MESH
        )

    sent = []

    def go(copy):
        copy.start()
        sent.append(copy)

    barrier = pltpu.get_barrier_semaphore()
    peers = [pair, sib, near, far] + [xpeer(o) for o in (1, 2, 3)] + [ypeer(o) for o in (1, 3)]
    for dev in peers:
        pl.semaphore_signal(barrier, inc=1, device_id=dev, device_id_type=MESH)
    pl.semaphore_wait(barrier, len(peers))

    kv_pair = rcopy(kv_ref, kvbuf.at[c, :, h], s_kv.at[0], r_kvz, pair)
    kv_pair.start()

    def kv_own(o):
        return rcopy(kv_ref, kvbuf.at[c, :, h], s_kv.at[o], r_kvx.at[o - 1, 0], xpeer(o))

    def kv_fwd(o):
        return rcopy(
            kvbuf.at[c, :, hp], kvbuf.at[c, :, hp], s_kv.at[3 + o], r_kvx.at[o - 1, 1], xpeer(o)
        )

    for o in (1, 2, 3):
        pl.when(c + o < NX)(lambda o=o: kv_own(o).start())
    kv_loc = pltpu.make_async_copy(kv_ref, kvbuf.at[c, :, h], loc.at[0])
    kv_loc.start()
    q_loc = pltpu.make_async_copy(q_ref.at[:, h], qown, loc.at[1])
    q_loc.start()
    w_loc = pltpu.make_async_copy(w_ref, wbuf.at[h, c], loc.at[2])
    w_loc.start()
    ein_loc = pltpu.make_async_copy(ein_ref, einbuf.at[:, h], loc.at[3])
    ein_loc.start()
    ed_loc = pltpu.make_async_copy(ed_ref, edbuf.at[h], loc.at[4])
    ed_loc.start()

    w_pair = rcopy(w_ref.at[k], wbuf.at[h, c, k], s_w.at[0], r_wz, pair)

    vext[:, :, HD:] = jnp.ones((NX, 1024, HD), BF)

    def spread_q(src, which, heads):
        for b in range(4):
            block = src[b]
            for n, j in enumerate(heads):
                q2[which, j, b] = block[:, n * HD : (n + 1) * HD]

    q_loc.wait()
    spread_q(qown, h, range(4))

    def q_pair(n):
        return rcopy(
            q_ref.at[:, hp, :, pl.ds(256 * n, 256)], qother.at[n], s_q.at[n], r_q.at[n], pair
        )

    kv_loc.wait()
    kv_pair.wait_recv()
    for o in (1, 2, 3):
        pl.when(c + o < NX)(lambda o=o: kv_fwd(o).start())
    go(q_pair(0))
    go(w_pair)
    go(q_pair(1))

    def put_v(src):
        vext[src, :, :HD] = kvbuf[src, 1].reshape(HD, 1024).astype(F32).T.astype(BF)

    put_v(c)
    def w_own(o):
        return rcopy(w_ref.at[k], wbuf.at[h, c, k], s_w.at[o], r_wx.at[o // 2, 0], xpeer(o))

    def w_fwd(o):
        part = wbuf.at[hp, c, k]
        return rcopy(part, part, s_w.at[3 + o], r_wx.at[o // 2, 1], xpeer(o))

    def w_opp(side, which):
        part = wbuf.at[hp if which else h, lax.rem(c + 3 - 2 * side, NX), k, side]
        return rcopy(
            part, part, s_wo.at[side, which], r_wo.at[side, which], xpeer(1 + 2 * side)
        )

    w_sib = rcopy(wbuf.at[hp, c, k], wbuf.at[hp, c, k], s_w.at[7], r_ws.at[0], sib)

    def w_sib_own(o):
        cs = lax.rem(c + NX - o, NX)
        return rcopy(wbuf.at[h, cs, k], wbuf.at[h, cs, k], s_w.at[7 + o], r_ws.at[o], sib)

    def w_sib_fwd(o):
        cs = lax.rem(c + NX - o, NX)
        return rcopy(wbuf.at[hp, cs, k], wbuf.at[hp, cs, k], s_w.at[10 + o], r_ws.at[3 + o], sib)

    def e_part(ref_in, ref_down, j, side):
        if j < 4:
            return ref_in.at[k, j] if side is None else ref_in.at[k, side, j]
        return ref_down.at[k, j - 4] if side is None else ref_down.at[side, k, j - 4]

    def e_across(j):
        return rcopy(
            e_part(ein_ref, ed_ref, j, None), e_part(einbuf, edbuf, j, h),
            s_e.at[0, j], r_e.at[j], far,
        )

    def e_inner(j):
        part = e_part(einbuf, edbuf, j, hp)
        return rcopy(part, part, s_e.at[1, j], r_e.at[j], near)

    def e_pass(j):
        @pl.when(edge)
        def _():
            e_across(j).wait_recv()
            e_inner(j).start()

    ein_sib = rcopy(einbuf.at[k, hp], einbuf.at[k, hp], s_sib.at[0], r_sib.at[0], sib)
    ed_sib = rcopy(edbuf.at[hp, k], edbuf.at[hp, k], s_sib.at[1], r_sib.at[1], sib)

    row_at = lax.broadcasted_iota(jnp.int32, (2, ROWS, 256), 1).reshape(2 * ROWS, 256) + h * ROWS
    col_at = lax.broadcasted_iota(jnp.int32, (2 * ROWS, 256), 1)
    allowed = col_at <= row_at

    def diagonal(which, j0):
        keys = kvbuf[c, 0].reshape(HD, 1024)
        for b in range(4):
            kl = (b + 1) * 256
            qs = q2[which, pl.ds(j0, 2), b].reshape(2 * ROWS, HD)
            s = jnp.dot(qs, keys[:, :kl], preferred_element_type=F32)
            last = jnp.where(allowed, s[:, kl - 256 :], -1e30)
            s = last if b == 0 else jnp.concatenate([s[:, : kl - 256], last], axis=1)
            top = jnp.broadcast_to(jnp.max(s, axis=1, keepdims=True) * SCALE2, (2 * ROWS, HD))
            p = jnp.exp2(s * SCALE2 - jnp.concatenate([top] * (kl // HD), axis=1)).astype(BF)
            acc[which, pl.ds(j0, 2), b] = jnp.dot(
                p, vext[c, :kl], preferred_element_type=F32
            ).reshape(2, ROWS, 2 * HD)
            mrow[which, pl.ds(j0, 2), b] = top.reshape(2, ROWS, HD)

    def full_block(which, j0, src):
        keys = kvbuf[src, 0].reshape(HD, 1024)
        for n in range(2):
            j = j0 + n
            qs = q2[which, j].reshape(4 * ROWS, HD)
            s = jnp.dot(qs, keys, preferred_element_type=F32)
            old = mrow[which, j].reshape(4 * ROWS, HD)
            top = jnp.maximum(old, jnp.max(s, axis=1, keepdims=True) * SCALE2)
            factor = jnp.exp2(old - top)
            p = jnp.exp2(s * SCALE2 - jnp.concatenate([top] * 8, axis=1)).astype(BF)
            update = jnp.dot(p, vext[src], preferred_element_type=F32)
            acc[which, j] = (
                acc[which, j].reshape(4 * ROWS, 2 * HD) * jnp.concatenate([factor] * 2, axis=1)
                + update
            ).reshape(4, ROWS, 2 * HD)
            mrow[which, j] = top.reshape(4, ROWS, HD)

    def group(g, carry):
        which = lax.rem(h + g // 2, 2)
        j0 = 2 * (g % 2)

        @pl.when(g == 2)
        def _():
            q_pair(0).wait_recv()
            spread_q(qother.at[0], hp, (0, 1))

        @pl.when(g == 3)
        def _():
            w_pair.wait_recv()
            for o in (1, 3):
                w_fwd(o).start()
            w_sib.start()
            q_pair(1).wait_recv()
            spread_q(qother.at[1], hp, (2, 3))

            @pl.when(edge)
            def _():
                for j in range(6):
                    e_across(j).start()

        diagonal(which, j0)

        def earlier(o, carry):
            src = c - o

            @pl.when(g == 0)
            def _():
                rcopy(
                    kv_ref, kvbuf.at[src, :, h], s_kv.at[o], r_kvx.at[o - 1, 0], xpeer(o)
                ).wait_recv()
                rcopy(
                    kv_ref, kvbuf.at[src, :, hp], s_kv.at[o], r_kvx.at[o - 1, 1], xpeer(o)
                ).wait_recv()
                put_v(src)

            full_block(which, j0, src)
            return carry

        lax.fori_loop(1, c + 1, earlier, 0)

        @pl.when(g == 0)
        def _():
            for o in (1, 2, 3):

                @pl.when(c + o < NX)
                def _(o=o):
                    kv_own(o).wait_send()
                    kv_fwd(o).wait_send()

            for o in (1, 3):
                w_own(o).start()

        return carry

    lax.fori_loop(0, 4, group, 0)

    for w in range(2):
        for j in range(4):
            whole = acc[w, j].reshape(4 * ROWS, 2 * HD)
            head = (whole[:, :HD] / whole[:, HD:]).astype(BF)
            att[:, :, (4 * w + j) * HD : (4 * w + j + 1) * HD] = head.reshape(4, ROWS, HD)

    for o in (1, 3):
        w_own(o).wait_recv()
        go(w_opp(o // 2, 0))
        w_sib_own(o).start()
    w_loc.wait()
    w_sib.wait_recv()

    def op_copy(i, side):
        return rcopy(
            sbuf.at[i, lax.rem(y + 2, NY), :, pl.ds(512 * side, 512)], oph.at[side, i],
            s_op.at[side, i], r_op.at[side, i], ypeer(1 + 2 * side),
        )

    def nb_copy(i, side):
        return rcopy(
            sbuf.at[i, lax.rem(y + 1 + 2 * side, NY)], rsbuf.at[side, i],
            s_rs.at[side, i], r_rs.at[side, i], ypeer(1 + 2 * side),
        )

    def add_own(i):
        for side in range(2):
            op_copy(i, side).wait_recv()
            to = lax.rem(y + 1 + 2 * side, NY)
            lo = 512 * side
            sbuf[i, to, :, lo : lo + 512] = (
                sbuf[i, to, :, lo : lo + 512].astype(F32) + oph[side, i].astype(F32)
            ).astype(BF)
            go(nb_copy(i, side))

    order = (0, 1, 3, 2)
    for i, o in enumerate(order):
        cs = lax.rem(c + NX - o, NX)
        if i == 1:
            for n in (1, 3):
                w_fwd(n).wait_recv()
                go(w_opp(n // 2, 1))
                w_sib_fwd(n).start()
        if i == 3:
            add_own(2)
            for which in range(2):
                for side in range(2):
                    w_opp(side, which).wait_recv()
            w_sib_own(o).start()
            w_sib_fwd(o).start()
        if i:
            w_sib_own(o).wait_recv()
            w_sib_fwd(o).wait_recv()

        def tile(n, carry, cs=cs, i=i):
            at = pl.ds(pl.multiple_of(n * 256, 256), 256)
            rows = att[...].reshape(4 * ROWS, 1024)
            w0 = wbuf[0, cs, :, :, :, at].reshape(512, 256)
            w1 = wbuf[1, cs, :, :, :, at].reshape(512, 256)
            part = jnp.dot(rows[:, :512], w0, preferred_element_type=F32)
            part = part + jnp.dot(rows[:, 512:], w1, preferred_element_type=F32)
            sbuf[i, :, :, at] = part.astype(BF).reshape(4, ROWS, 256)
            return carry

        lax.fori_loop(0, 4, tile, 0)
        for side in range(2):
            go(op_copy(i, side))
        if i in (1, 2):
            add_own(i - 1)
    add_own(3)
    e_pass(0)

    slot_at = lax.broadcasted_iota(jnp.int32, (ROWS, ROWS), 0)
    lane_at = lax.broadcasted_iota(jnp.int32, (ROWS, ROWS), 1)
    group_at = sum((slot_at >= n * CAP).astype(jnp.int32) for n in (1, 2, 3, 4))
    expert_at = group_at + c
    expert_at = jnp.where(expert_at >= NX, expert_at - NX, expert_at)
    expert_at = jnp.where(group_at == 4, -1, expert_at)
    match = jnp.zeros((ROWS, ROWS), F32)
    gate = jnp.zeros((ROWS, ROWS), F32)
    for n in range(8):
        hit = ids_ref[n : n + 1, :] == expert_at
        match = match + jnp.where(hit, 1.0, 0.0)
        gate = gate + jnp.where(hit, gw_ref[n : n + 1, :], 0.0)
    before = jnp.where(slot_at < lane_at, 1.0, 0.0).astype(BF)
    rank = jnp.dot(match.astype(BF), before, preferred_element_type=F32)
    want = (slot_at - group_at * CAP).astype(F32)
    chosen = jnp.where(rank == want, match, 0.0)
    weighted = (chosen * gate).T
    chosen = chosen.astype(BF)

    square = jnp.zeros((ROWS, 1), F32)
    for i, o in enumerate(order):
        cs = lax.rem(c + NX - o, NX)
        at = pl.ds(pl.multiple_of(cs * 1024, 1024), 1024)
        for side in range(2):
            nb_copy(i, side).wait_recv()
        total = sbuf[i, y].astype(F32) + rsbuf[0, i].astype(F32) + rsbuf[1, i].astype(F32)
        block = (res_ref[:, at].astype(F32) + total).astype(BF)
        stream[:, at] = block
        wide = block.astype(F32)
        square = square + jnp.sum(wide * wide, axis=1, keepdims=True)
        if i in (1, 3):
            e_pass(1 + i // 2)
    inv = lax.rsqrt(square * (1.0 / D) + 1e-6)

    def x_copy(half, o):
        return rcopy(
            packed.at[o, half], xd.at[o - 1, half], s_x.at[half, o - 1], r_x.at[half, o - 1], xpeer(o)
        )

    def y_copy(half, side):
        return rcopy(
            disp.at[half, 0], disp.at[half, 1 + side], s_y.at[half, side], r_y.at[half, side],
            ypeer(1 + 2 * side),
        )

    def y_pass(half):
        return rcopy(
            disp.at[half, 1 + half], disp.at[half, 3], s_yp.at[half], r_yp.at[half],
            ypeer(1 + 2 * half),
        )

    def merge(pieces, quarter, extra):
        lo = (quarter % 2) * CAP
        return jnp.concatenate([p[lo : lo + CAP] for p in pieces] + extra, axis=0).astype(BF)

    def split(rows, quarter):
        lo = (quarter % 2) * CAP
        for o in range(NX):
            xsend[o, lo : lo + CAP] = rows[o * CAP : (o + 1) * CAP]

    for half in range(2):
        for quarter in (2 * half, 2 * half + 1):
            at = slice(quarter * 1024, (quarter + 1) * 1024)
            normed = (stream[:, at].astype(F32) * inv * gain_ref[:, at]).astype(BF)
            split(jnp.dot(chosen, normed, preferred_element_type=F32), quarter)
        packed[:, half] = xsend[...].astype(BF)
        for o in (2, 1, 3):
            go(x_copy(half, o))
    e_pass(3)
    for half in range(2):
        for o in (1, 3, 2):
            x_copy(half, o).wait_recv()
        pieces = [packed[0, half].astype(F32)] + [xd[o, half].astype(F32) for o in range(3)]
        for n in range(2):
            disp[half, 0, :, n * 1024 : (n + 1) * 1024] = merge(pieces, n, [])
        for side in range(2):
            go(y_copy(half, side))
        e_pass(4 + half)

    @pl.when(jnp.logical_not(edge))
    def _():
        for j in range(6):
            e_inner(j).wait_recv()

    go(ein_sib)
    go(ed_sib)
    y_copy(0, 0).wait_recv()
    go(y_pass(0))
    y_copy(1, 1).wait_recv()
    go(y_pass(1))
    ein_loc.wait()
    ed_loc.wait()
    ein_sib.wait_recv()
    ed_sib.wait_recv()

    def project_in(n, half, lo_slot, hi_slot):
        rows = (hi_slot - lo_slot) * EROWS
        total = jnp.zeros((rows, 384), F32)
        for kk in range(2):
            lo = kk * 1024
            at = half * HALF + lo
            total = total + lax.dot_general(
                disp[half, lo_slot:hi_slot, :, lo : lo + 1024].reshape(rows, 1024),
                einbuf[n, :, :, :, at : at + 1024].reshape(384, 1024),
                NT,
                preferred_element_type=F32,
            )
        return total

    y_copy(0, 1).wait_recv()
    y_pass(0).wait_recv()
    parts = [project_in(n, 0, 0, 4) for n in range(2)]
    y_copy(1, 0).wait_recv()
    parts_near = [project_in(n, 1, 0, 3) for n in range(2)]
    y_pass(1).wait_recv()
    gate_part, up_part = [
        parts[n] + jnp.concatenate([parts_near[n], project_in(n, 1, 3, 4)], axis=0)
        for n in range(2)
    ]
    hidden = (gate_part / (1.0 + jnp.exp(-gate_part)) * up_part).astype(BF)

    def ro_copy(half):
        return rcopy(
            down.at[half, 3], rop.at[half], s_ro.at[half], r_ro.at[half], ypeer(1 + 2 * half)
        )

    def rn_copy(half, side):
        return rcopy(
            down.at[half, 2 - side], rnb.at[half, side], s_rn.at[half, side],
            r_rn.at[half, side], ypeer(1 + 2 * side),
        )

    for half in range(2):

        def down_tile(n, carry, half=half):
            lo = pl.multiple_of(n * 512, 512)
            weights = edbuf[:, :, :, :, pl.ds(half * HALF + lo, 512)].reshape(384, 512)
            part = jnp.dot(hidden, weights, preferred_element_type=F32)
            down[half, :, :, pl.ds(lo, 512)] = part.astype(BF).reshape(4, EROWS, 512)
            return carry

        lax.fori_loop(0, HALF // 512, down_tile, 0)
        if half == 0:
            go(ro_copy(0))
            go(rn_copy(0, 1))
        else:
            go(ro_copy(1))
    for half in range(2):
        ro_copy(half).wait_recv()
        slot = 2 - half
        down[half, slot] = (down[half, slot].astype(F32) + rop[half].astype(F32)).astype(BF)
        go(rn_copy(half, half))
        if half == 0:
            go(rn_copy(1, 0))

    def rx_copy(half, o):
        return rcopy(
            back.at[o, half], eb.at[o - 1, half], s_rx.at[half, o - 1], r_rx.at[half, o - 1],
            xpeer(NX - o),
        )

    for half in range(2):
        for side in range(2):
            rn_copy(half, side).wait_recv()
        for n in range(2):
            at = slice(n * 1024, (n + 1) * 1024)
            total = down[half, 0, :, at].astype(F32)
            for side in range(2):
                total = total + rnb[half, side, :, at].astype(F32)
            split(total, n)
        back[:, half] = xsend[...].astype(BF)
        for o in (2, 1, 3):
            go(rx_copy(half, o))
    high = weighted.astype(BF)
    rest = weighted - high.astype(F32)
    mid = rest.astype(BF)
    low = (rest - mid.astype(F32)).astype(BF)
    for half in range(2):
        for o in (1, 3, 2):
            rx_copy(half, o).wait_recv()
        pieces = [back[0, half].astype(F32)] + [eb[o, half].astype(F32) for o in range(3)]
        for n in range(2):
            at = slice(half * HALF + n * 1024, half * HALF + (n + 1) * 1024)
            rows = merge(pieces, n, [jnp.zeros((ROWS - EROWS, 1024), F32)])
            added = (
                jnp.dot(high, rows, preferred_element_type=F32)
                + jnp.dot(mid, rows, preferred_element_type=F32)
                + jnp.dot(low, rows, preferred_element_type=F32)
            )
            out_ref[:, at] = (stream[:, at].astype(F32) + added).astype(BF)

    kv_pair.wait_send()
    w_sib.wait_send()
    for o in (1, 2, 3):
        if o != 2:
            w_own(o).wait_send()
            w_fwd(o).wait_send()
        w_sib_own(o).wait_send()
        w_sib_fwd(o).wait_send()

    @pl.when(edge)
    def _():
        for j in range(6):
            e_across(j).wait_send()
            e_inner(j).wait_send()

    for copy in sent:
        copy.wait_send()


def body(residual, queries, key_value, out_proj, norm_gain, expert_ids, gate_weights, expert_in, expert_down):
    sem = pltpu.SemaphoreType.DMA
    vmem = pl.BlockSpec(memory_space=pltpu.VMEM)
    hbm = pl.BlockSpec(memory_space=pl.ANY)
    scratch = [
        pltpu.VMEM((NX, 2, 2, 64, 1024), BF),
        pltpu.VMEM((NX, 1024, 2 * HD), BF),
        pltpu.VMEM((2, 4, 4, ROWS, HD), BF),
        pltpu.VMEM((4, ROWS, 512), BF),
        pltpu.VMEM((2, 4, ROWS, 256), BF),
        pltpu.VMEM((2, 4, 4, ROWS, 2 * HD), F32),
        pltpu.VMEM((2, 4, 4, ROWS, HD), F32),
        pltpu.VMEM((4, ROWS, 1024), BF),
        pltpu.VMEM((2, NX, 2, 2, ROWS, 1024), BF),
        pltpu.VMEM((4, NY, ROWS, 1024), BF),
        pltpu.VMEM((2, 4, ROWS, 512), BF),
        pltpu.VMEM((2, 4, ROWS, 1024), BF),
        pltpu.VMEM((ROWS, D), BF),
        pltpu.VMEM((NX, 2 * CAP, 1024), F32),
        pltpu.VMEM((NX, 2, 2 * CAP, 1024), BF),
        pltpu.VMEM((3, 2, 2 * CAP, 1024), BF),
        pltpu.VMEM((2, NY, EROWS, HALF), BF),
        pltpu.VMEM((2, NY, EROWS, HALF), BF),
        pltpu.VMEM((2, EROWS, HALF), BF),
        pltpu.VMEM((2, 2, EROWS, HALF), BF),
        pltpu.VMEM((NX, 2, 2 * CAP, 1024), BF),
        pltpu.VMEM((3, 2, 2 * CAP, 1024), BF),
        pltpu.VMEM((2, 2, 4, 48, D), BF),
        pltpu.VMEM((2, 2, 2, 48, D), BF),
        sem((5,)),
        sem((7,)), sem, sem((3, 2)),
        sem((2,)), sem((2,)),
        sem((14,)), sem, sem((2, 2)), sem((2, 2)), sem((2, 2)), sem((7,)),
        sem((2, 4)), sem((2, 4)), sem((2, 4)), sem((2, 4)),
        sem((2, 6)), sem((6,)), sem((2,)), sem((2,)),
        sem((2, 3)), sem((2, 3)), sem((2, 2)), sem((2, 2)), sem((2,)), sem((2,)),
        sem((2,)), sem((2,)), sem((2, 2)), sem((2, 2)), sem((2, 3)), sem((2, 3)),
    ]
    return pl.pallas_call(
        kernel,
        out_shape=jax.ShapeDtypeStruct((ROWS, D), BF),
        in_specs=[hbm, hbm, hbm, vmem, vmem, vmem, vmem, hbm, hbm],
        out_specs=vmem,
        scratch_shapes=scratch,
        compiler_params=pltpu.CompilerParams(
            collective_id=0, has_side_effects=True, vmem_limit_bytes=62 * 1024 * 1024
        ),
        name="layer",
    )(
        queries.reshape(4, 2, ROWS, 512),
        jnp.swapaxes(key_value, 1, 2),
        out_proj.reshape(2, 2, ROWS, 1024),
        residual,
        norm_gain.reshape(1, D),
        expert_ids.T,
        gate_weights.T,
        jnp.swapaxes(expert_in[0], 1, 2).reshape(2, 4, 48, D),
        expert_down[0].reshape(2, 2, 48, D),
    )


def solution(mesh):
    in_specs = (
        P(("dp", "ctx", "tp"), None),
        P(("dp", "ctx"), "tp"),
        P(None, ("dp", "ctx"), "tp"),
        P("tp", "ctx"),
        P(),
        P(("dp", "ctx", "tp"), None),
        P(("dp", "ctx", "tp"), None),
        P("ctx", None, None, "tp"),
        P("ctx", "tp", None),
    )
    out_specs = P(("dp", "ctx", "tp"), None)
    return jax.shard_map(body, mesh=mesh, in_specs=in_specs, out_specs=out_specs, check_vma=False)
```
